512 devices in a mesh: phase: 8 (over z), ctx: 64 (over x, y, core).
Axes of the slice: x: 4, y: 8, z: 8, core: 2. Of those that a mesh axis runs over, the one named last changes fastest.
Arguments:
- activations: bfloat16 [8, 8192, 4096], P('phase', 'ctx'), may hold values from -6 to 6
- norm_gain: bfloat16 [8, 4096], P('phase'), may hold values from 0.25 to 1.75
- short_taps: bfloat16 [8, 3, 3, 4096], P('phase'), may hold values from -3 to 3
- skip_gain: bfloat16 [8, 4096], P('phase'), may hold values from 0.19921875 to 1.5
- time_const: float32 [8, 4096, 16], P('phase', 'ctx'), may hold values from 25 to 32768
- residues: float32 [8, 4096, 16], P('phase', 'ctx'), may hold values from -2 to 2
Outputs:
- handed: bfloat16 [8, 8192, 4096], P('phase', 'ctx')
The draws below stay inside these ranges and needn't reach their ends.
All inputs are finite; a program needn't handle non-finite values.
Results may differ from the reference program's by a relative error of at most 0.0058.
Values may be sent and summed in bfloat16 or wider, within the bound.
A program may use at most 128 MiB of HBM per device.

```python
import math
import jax
import jax.numpy as jnp
from jax import lax

C = 4096
MODES = 16
SEQ = 8192
PHASES = 8


def draw_activations(key, part):
    key = jax.random.fold_in(key, 11)
    value_key, token_key, channel_key = jax.random.split(key, 3)
    token_scale = jnp.exp(jax.random.uniform(token_key, (PHASES, SEQ, 1), jnp.float32, math.log(0.2), math.log(2.0)))
    channel_scale = jnp.exp(jax.random.uniform(channel_key, (PHASES, 1, C), jnp.float32, math.log(0.6), math.log(1.6)))
    raw_values = jnp.clip(jax.random.normal(value_key, (PHASES, SEQ, C), jnp.float32), -3.0, 3.0)
    return jnp.clip(raw_values * token_scale * channel_scale, -6.0, 6.0).astype(jnp.bfloat16)


def draw_time_const(key, part):
    key = jax.random.fold_in(key, 23)
    slow_key, fast_key, pick_key = jax.random.split(key, 3)
    shape = (PHASES, C, MODES)
    slow_times = jnp.exp(jax.random.uniform(slow_key, shape, jnp.float32, math.log(SEQ / 2.0), math.log(4.0 * SEQ)))
    fast_times = jnp.exp(jax.random.uniform(fast_key, shape, jnp.float32, math.log(25.0), math.log(SEQ / 2.0)))
    chosen = jax.random.bernoulli(pick_key, 0.5, shape)
    return jnp.clip(jnp.where(chosen, slow_times, fast_times), 25.0, 4.0 * SEQ).astype(jnp.float32)


def steps_of(rng, extent, cuts, low, high):
    level = 1.0
    for dim, shards_of in cuts:
        draws = jax.random.uniform(jax.random.fold_in(jax.random.fold_in(rng, 6), dim), (shards_of,), jnp.float32, low / len(cuts), high / len(cuts))
        level = level * jnp.repeat(jnp.exp(draws), extent[dim] // shards_of).reshape((-1,) + (1,) * (len(extent) - 1 - dim))
    return level


def scatter_about(own_key, dims, spread, most, cuts=(), kind=jnp.bfloat16):
    loudness = steps_of(own_key, dims, cuts, -0.22, 0.18) if cuts else 1.0
    values = jax.random.normal(own_key, dims, jnp.float32) * spread * loudness
    return jnp.minimum(jnp.maximum(values, -most), most).astype(kind)


def setup_inputs(seed: int = 0) -> dict:
    arg_keys = jax.random.split(jax.random.key(seed), 7)
    return {
        "activations": draw_activations(jax.random.fold_in(arg_keys[6], 71), 0),
        "norm_gain": jnp.clip(1.0 + 0.15 * jax.random.normal(arg_keys[1], (PHASES, C), jnp.float32), 0.25, 1.75).astype(jnp.bfloat16),
        "short_taps": scatter_about(arg_keys[2], (PHASES, 3, 3, C), 0.5, 3.0, ((0, 8),)),
        "skip_gain": jnp.clip(0.19921875 + 1.3007812 * jax.random.uniform(arg_keys[3], (PHASES, C), jnp.float32) ** steps_of(arg_keys[3], (PHASES, C), ((0, 8),), -0.2, 0.2), 0.19921875, 1.5).astype(jnp.bfloat16),
        "time_const": draw_time_const(jax.random.fold_in(arg_keys[6], 71), 0),
        "residues": scatter_about(arg_keys[5], (PHASES, C, MODES), 0.3, 2.0, ((0, 8), (1, 64)), jnp.float32),
    }


def long_convolution(mixed_in, decay_time, residue):
    length, channels = mixed_in.shape
    group_size = 64
    group_count = channels // group_size
    padded_length = 2 * length
    position = jnp.arange(length, dtype=jnp.float32)
    lines = jnp.transpose(mixed_in.astype(jnp.float32)).reshape(group_count, group_size, length)
    time_groups = decay_time.reshape(group_count, group_size, -1)
    residue_groups = residue.reshape(group_count, group_size, -1)

    def one_group(pieces):
        signal, times, weights = pieces
        powers = jnp.exp(-position[None, None, :] / times[:, :, None])
        scaled = weights * jnp.sqrt(-jnp.expm1(-2.0 / times))
        response = lax.optimization_barrier(jnp.sum(scaled[:, :, None] * powers, axis=1))
        product = jnp.fft.rfft(signal, n=padded_length) * jnp.fft.rfft(response, n=padded_length)
        return jnp.fft.irfft(product, n=padded_length)[:, :length]
    result = lax.map(one_group, (lines, time_groups, residue_groups))
    return jnp.transpose(result.reshape(channels, length))

def hyena_block(inputs, gain, taps, skip, decay_time, residue):
    length = inputs.shape[0]
    wide_in = inputs.astype(jnp.float32)
    square_mean = lax.optimization_barrier(jnp.mean(wide_in * wide_in, axis=-1, keepdims=True))
    normed = (wide_in * lax.rsqrt(square_mean + 1e-06) * gain.astype(jnp.float32)).astype(jnp.bfloat16)
    padded = jnp.concatenate([jnp.zeros((2, inputs.shape[1]), jnp.bfloat16), normed], axis=0)
    wide_taps = taps.astype(jnp.float32)
    features = []
    for branch in range(3):
        total = jnp.zeros(inputs.shape, jnp.float32)
        for offset in range(3):
            total = total + wide_taps[branch, offset][None, :] * padded[2 - offset:2 - offset + length].astype(jnp.float32)
        features.append(total)
    query_feat, key_feat, value_feat = features
    mixed_in = (key_feat * value_feat).astype(jnp.bfloat16)
    conv_out = long_convolution(mixed_in, decay_time, residue).astype(jnp.bfloat16)
    direct = skip.astype(jnp.float32)[None, :] * mixed_in.astype(jnp.float32)
    return (wide_in + query_feat * (conv_out.astype(jnp.float32) + direct)).astype(jnp.bfloat16)

def reference(activations, norm_gain, short_taps, skip_gain, time_const, residues):
    outputs = []
    for section in range(activations.shape[0]):
        outputs.append(hyena_block(activations[section], norm_gain[section], short_taps[section], skip_gain[section], time_const[section], residues[section]))
    stacked = jnp.stack(outputs, axis=0)
    return jnp.roll(stacked, 1, axis=0)
```

```python
import functools

import jax
import jax.numpy as jnp
from jax import lax
from jax.experimental import pallas as pl
from jax.experimental.pallas import tpu as pltpu
from jax.sharding import PartitionSpec as P

MESH = pl.DeviceIdType.MESH
LANES = 128
MODES = 16
ROWS = 8
CORES = 2
F32 = jnp.float32
BF16 = jnp.bfloat16


def drain(ref, sem):
    pltpu.make_async_copy(ref, ref, sem).wait()


def kernel(
    phases, nx, tokens, act, prm, blk, out,
    halo, mate, raw, inv, par, rate, wgt, av, wv, qf, uu, ob,
    sb, rb, pb, cb, rt, rx,
    halo_sem, mate_sem, px_sem, py_sem, row_sem, tot_sem, car_sem, z_sem,
):
    nyc = ROWS * CORES
    ctx = nx * nyc
    groups = nx * ROWS
    channels = groups * LANES
    halves = nx // 2
    phase = lax.axis_index("phase")
    me = lax.axis_index("ctx")
    x = me // nyc
    yc = lax.rem(me, nyc)
    y = yc // CORES
    c = lax.rem(yc, CORES)
    after = lax.rem(me + 1, ctx)
    before = lax.rem(me + ctx - 1, ctx)
    above = lax.rem(phase + 1, phases)
    below = lax.rem(phase + phases - 1, phases)

    barrier = pltpu.get_barrier_semaphore()

    def greet_row(p, carry):
        peer = x * nyc + lax.rem(yc + p, nyc)
        pl.semaphore_signal(barrier, inc=1, device_id={"ctx": peer}, device_id_type=MESH)
        return carry

    lax.fori_loop(1, nyc, greet_row, 0)

    def greet_col(p, carry):
        peer = lax.rem(x + p, nx) * nyc + yc
        pl.semaphore_signal(barrier, inc=1, device_id={"ctx": peer}, device_id_type=MESH)
        return carry

    lax.fori_loop(1, nx, greet_col, 0)
    pl.semaphore_signal(barrier, inc=1, device_id={"ctx": before}, device_id_type=MESH)
    pl.semaphore_signal(barrier, inc=1, device_id={"phase": below}, device_id_type=MESH)
    pl.semaphore_wait(barrier, nyc - 1 + nx - 1 + 2)

    def send(src, dst, sems, where):
        pltpu.make_async_remote_copy(
            src_ref=src, dst_ref=dst, send_sem=sems.at[0], recv_sem=sems.at[1],
            device_id=where, device_id_type=MESH,
        ).start()

    def send_row(src, dst, sems):
        def one(p, carry):
            j = lax.rem(yc + p, nyc)
            send(src.at[pl.ds(j * MODES, MODES)], dst.at[pl.ds(yc * MODES, MODES)],
                 sems, {"ctx": x * nyc + j})
            return carry
        lax.fori_loop(1, nyc, one, 0)

    def send_col(src, dst, sems):
        def one(p, carry):
            peer = lax.rem(x + p, nx) * nyc + yc
            send(src, dst, sems, {"ctx": peer})
            return carry
        lax.fori_loop(1, nx, one, 0)

    send(blk, mate, mate_sem, {"ctx": x * nyc + y * CORES + (1 - c)})
    send(act.at[pl.ds(tokens - 16, 16)], halo, halo_sem, {"ctx": after})

    for g in range(groups):
        tile = prm[:, g * LANES:(g + 1) * LANES].astype(F32)
        par[pl.ds(g, 8, stride=groups), :] = tile[:8]
        par[pl.ds(8 * groups + g, 8, stride=groups), :] = tile[8:]

    drain(mate, mate_sem.at[1])
    slot = pl.ds((y * nx + x) * MODES, MODES)
    rate[slot, :] = blk[0:MODES, :] + mate[0:MODES, :]
    wgt[slot, :] = blk[MODES:2 * MODES, :] + mate[MODES:2 * MODES, :]
    send_col(rate.at[slot], rate.at[slot], px_sem.at[0])
    send_col(wgt.at[slot], wgt.at[slot], px_sem.at[1])

    def spread(tile_ref, source, place):
        total = jnp.zeros((16, LANES), F32)
        for g in range(groups):
            tile = tile_ref[pl.ds(source, 16), g * LANES:(g + 1) * LANES].astype(F32)
            raw[pl.ds(place * groups + g, 8, stride=groups), :] = tile[:8]
            raw[pl.ds((place + 8) * groups + g, 8, stride=groups), :] = tile[8:]
            total = total + tile * tile
        mean = jnp.sum(total, axis=1, keepdims=True) * (1.0 / channels)
        inv[pl.ds(place, 16), :] = jnp.broadcast_to(lax.rsqrt(mean + 1e-06), (16, LANES))

    def spread_own(i, carry):
        start = pl.multiple_of(i * 16, 16)
        spread(act, start, start + 16)
        return carry

    lax.fori_loop(0, tokens // 16, spread_own, 0)

    drain(rate.at[pl.ds(0, (nx - 1) * MODES)], px_sem.at[0, 1])
    drain(wgt.at[pl.ds(0, (nx - 1) * MODES)], px_sem.at[1, 1])
    line = pl.ds(y * nx * MODES, nx * MODES)

    def send_line(array, sems):
        def one(p, carry):
            peer = x * nyc + lax.rem(y + p, ROWS) * CORES + c
            send(array.at[line], array.at[line], sems, {"ctx": peer})
            return carry
        lax.fori_loop(1, ROWS, one, 0)

    send_line(rate, py_sem.at[0])
    send_line(wgt, py_sem.at[1])

    drain(halo, halo_sem.at[1])
    spread(halo, 0, 0)

    def rows_of(token, q):
        return pl.ds(pl.multiple_of(token * groups + 8 * q, 8), 8)

    first = jnp.where(me > 0, 1.0, 0.0).astype(F32)

    def features(q):
        gain = par[8 * q:8 * q + 8, :]
        taps = [par[(1 + j) * groups + 8 * q:(1 + j) * groups + 8 * q + 8, :] for j in range(9)]

        def normed(token):
            wide = raw[rows_of(token, q), :] * inv[pl.ds(token, 1), :] * gain
            return wide.astype(BF16).astype(F32)

        def one(i, carry):
            back1, back2 = carry
            for k in range(4):
                t = i * 4 + k
                now = normed(t + 16)
                feats = [
                    (taps[3 * b] * now + taps[3 * b + 1] * back1) + taps[3 * b + 2] * back2
                    for b in range(3)
                ]
                qf[rows_of(t, q), :] = feats[0]
                uu[rows_of(t, q), :] = (feats[1] * feats[2]).astype(BF16).astype(F32)
                back1, back2 = now, back1
            return back1, back2

        lax.fori_loop(0, tokens // 4, one, (normed(15) * first, normed(14) * first))

    for q in range(nx):
        features(q)

    drain(rate.at[pl.ds(0, (ROWS - 1) * nx * MODES)], py_sem.at[0, 1])
    for q in range(nx):
        for r in range(MODES):
            value = rate[pl.ds(q * MODES + r, 8, stride=nx * MODES), :]
            av[r * groups + 8 * q:r * groups + 8 * q + 8, :] = jnp.exp(-value)

    def end_state(h):
        for k in range(2):
            q = 2 * h + k
            decay = [av[r * groups + 8 * q:r * groups + 8 * q + 8, :] for r in range(MODES)]

            def one(i, state):
                for step in range(4):
                    value = uu[rows_of(i * 4 + step, q), :]
                    state = tuple(decay[r] * state[r] + value for r in range(MODES))
                return state

            state = lax.fori_loop(
                0, tokens // 4, one, tuple(jnp.zeros((8, LANES), F32) for _ in range(MODES))
            )
            for r in range(MODES):
                sb[h, pl.ds(k * MODES + r, 8, stride=CORES * MODES), :] = state[r]
        send_row(sb.at[h], rb.at[h], row_sem.at[h])
        own = pl.ds(yc * MODES, MODES)
        rb[h, own, :] = sb[h, own, :]

    for h in range(halves):
        end_state(h)

    def own_rate(h):
        return rate[pl.ds((y * nx + 2 * h + c) * MODES, MODES), :]

    for h in range(halves):
        drain(rb.at[h, pl.ds(0, (nyc - 1) * MODES)], row_sem.at[h, 1])
        shard_decay = jnp.exp(own_rate(h) * (-float(tokens)))
        state = jnp.zeros((MODES, LANES), F32)
        for j in range(nyc):
            pb[h, j * MODES:(j + 1) * MODES, :] = state
            state = shard_decay * state + rb[h, j * MODES:(j + 1) * MODES, :]
        rt[h] = state
        rx[h, pl.ds(x * MODES, MODES), :] = state
        send_col(rt.at[h], rx.at[h, pl.ds(x * MODES, MODES)], tot_sem.at[h])

    drain(wgt.at[pl.ds(0, (ROWS - 1) * nx * MODES)], py_sem.at[1, 1])
    for q in range(nx):
        for r in range(MODES):
            wv[r * groups + 8 * q:r * groups + 8 * q + 8, :] = (
                wgt[pl.ds(q * MODES + r, 8, stride=nx * MODES), :])

    for h in range(halves):
        drain(rx.at[h, pl.ds(0, (nx - 1) * MODES)], tot_sem.at[h, 1])
        shard_decay = jnp.exp(own_rate(h) * (-float(tokens)))
        line_decay = jnp.exp(own_rate(h) * (-float(tokens * nyc)))
        enter = jnp.zeros((MODES, LANES), F32)
        for k in range(nx):
            earlier = jnp.broadcast_to(jnp.where(k < x, 1.0, 0.0).astype(F32), (MODES, LANES))
            longer = line_decay * enter + rx[h, k * MODES:(k + 1) * MODES, :]
            enter = jnp.where(earlier > 0.5, longer, enter)
        for j in range(nyc):
            pb[h, j * MODES:(j + 1) * MODES, :] += enter
            enter = enter * shard_decay
        send_row(pb.at[h], cb.at[h], car_sem.at[h])
        own = pl.ds(yc * MODES, MODES)
        cb[h, own, :] = pb[h, own, :]

    def finish(h, k):
        q = 2 * h + k
        decay = [av[r * groups + 8 * q:r * groups + 8 * q + 8, :] for r in range(MODES)]
        weight = [wv[r * groups + 8 * q:r * groups + 8 * q + 8, :] for r in range(MODES)]
        skip = par[10 * groups + 8 * q:10 * groups + 8 * q + 8, :]

        def one(i, state):
            for step in range(4):
                t = i * 4 + step
                value = uu[rows_of(t, q), :]
                state = tuple(decay[r] * state[r] + value for r in range(MODES))
                terms = [weight[r] * state[r] for r in range(MODES)]
                while len(terms) > 1:
                    terms = [terms[2 * m] + terms[2 * m + 1] for m in range(len(terms) // 2)]
                conv = terms[0].astype(BF16).astype(F32)
                qf[rows_of(t, q), :] = (
                    raw[rows_of(t + 16, q), :]
                    + qf[rows_of(t, q), :] * (conv + skip * value))
            return state

        state = tuple(
            cb[h, pl.ds(k * MODES + r, 8, stride=CORES * MODES), :] for r in range(MODES))
        lax.fori_loop(0, tokens // 4, one, state)

        def gather(i, carry):
            start = pl.multiple_of(i * 16, 16)
            for g in range(8 * q, 8 * q + 8):
                low = qf[pl.ds(start * groups + g, 8, stride=groups), :]
                high = qf[pl.ds((start + 8) * groups + g, 8, stride=groups), :]
                ob[pl.ds(start, 16), g * LANES:(g + 1) * LANES] = (
                    jnp.concatenate([low, high], axis=0).astype(BF16))
            return carry

        lax.fori_loop(0, tokens // 16, gather, 0)
        part = pl.ds(q * 8 * LANES, 8 * LANES)
        send(ob.at[:, part], out.at[:, part], z_sem, {"phase": above})

    for h in range(halves):
        drain(cb.at[h, pl.ds(0, (nyc - 1) * MODES)], car_sem.at[h, 1])
        for k in range(2):
            finish(h, k)

    drain(blk, mate_sem.at[0])
    drain(halo, halo_sem.at[0])
    for k, array in enumerate((rate, wgt)):
        drain(array.at[pl.ds(0, (nx - 1) * MODES)], px_sem.at[k, 0])
        drain(array.at[pl.ds(0, (ROWS - 1) * nx * MODES)], py_sem.at[k, 0])
    for h in range(halves):
        drain(rb.at[h, pl.ds(0, (nyc - 1) * MODES)], row_sem.at[h, 0])
        drain(rx.at[h, pl.ds(0, (nx - 1) * MODES)], tot_sem.at[h, 0])
        drain(rb.at[h, pl.ds(0, (nyc - 1) * MODES)], car_sem.at[h, 0])
    drain(ob, z_sem.at[0])
    drain(ob, z_sem.at[1])


def local(phases, nx, activations, norm_gain, short_taps, skip_gain, time_const, residues):
    act = activations[0]
    tokens, channels = act.shape
    groups = channels // LANES
    halves = nx // 2
    nyc = ROWS * CORES
    prm = jnp.concatenate(
        [norm_gain, short_taps[0].reshape(9, channels), skip_gain,
         jnp.zeros((5, channels), BF16)], axis=0)
    rate = 1.0 / time_const[0]
    weight = residues[0] * jnp.sqrt(-jnp.expm1(-2.0 * rate))
    both = jnp.concatenate([rate.T, weight.T], axis=0)
    wide = jnp.concatenate([both, both], axis=1)
    half = LANES // CORES
    column = lax.broadcasted_iota(jnp.int32, wide.shape, 1) // half
    blk = jnp.where(column == lax.axis_index("ctx") % CORES, wide, 0.0)
    vmem = pltpu.VMEM
    dma = pltpu.SemaphoreType.DMA
    out = pl.pallas_call(
        functools.partial(kernel, phases, nx, tokens),
        out_shape=jax.ShapeDtypeStruct((tokens, channels), BF16),
        in_specs=[pl.BlockSpec(memory_space=vmem)] * 3,
        out_specs=pl.BlockSpec(memory_space=pl.ANY),
        scratch_shapes=[
            vmem((16, channels), BF16),
            vmem((2 * MODES, LANES), F32),
            vmem(((tokens + 16) * groups, LANES), F32),
            vmem((tokens + 16, LANES), F32),
            vmem((16 * groups, LANES), F32),
            vmem((groups * MODES, LANES), F32),
            vmem((groups * MODES, LANES), F32),
            vmem((groups * MODES, LANES), F32),
            vmem((groups * MODES, LANES), F32),
            vmem((tokens * groups, LANES), F32),
            vmem((tokens * groups, LANES), F32),
            vmem((tokens, channels), BF16),
            vmem((halves, nyc * MODES, LANES), F32),
            vmem((halves, nyc * MODES, LANES), F32),
            vmem((halves, nyc * MODES, LANES), F32),
            vmem((halves, nyc * MODES, LANES), F32),
            vmem((halves, MODES, LANES), F32),
            vmem((halves, nx * MODES, LANES), F32),
            dma((2,)),
            dma((2,)),
            dma((2, 2)),
            dma((2, 2)),
            dma((halves, 2)),
            dma((halves, 2)),
            dma((halves, 2)),
            dma((2,)),
        ],
        compiler_params=pltpu.CompilerParams(
            collective_id=0, has_side_effects=True, vmem_limit_bytes=40 * 1024 * 1024),
    )(act, prm, blk)
    return out[None]


def solution(mesh):
    in_specs = (
        P("phase", "ctx", None),
        P("phase", None),
        P("phase", None, None, None),
        P("phase", None),
        P("phase", "ctx", None),
        P("phase", "ctx", None),
    )
    nx = mesh.shape["ctx"] // (ROWS * CORES)
    return jax.shard_map(
        functools.partial(local, mesh.shape["phase"], nx),
        mesh=mesh, in_specs=in_specs, out_specs=P("phase", "ctx", None), check_vma=False)
```

```python
import functools

import jax
import jax.numpy as jnp
from jax import lax
from jax.experimental import pallas as pl
from jax.experimental.pallas import tpu as pltpu
from jax.sharding import PartitionSpec as P

MESH = pl.DeviceIdType.MESH
LANES = 128
MODES = 16
ROWS = 8
CORES = 2
NEAR = 1
PLAN = (
    (),
    ((2, 0, 128),),
    ((3, 0, 128),),
    (),
    (),
)
F32 = jnp.float32
BF16 = jnp.bfloat16


def drain(ref, sem):
    pltpu.make_async_copy(ref, ref, sem).wait()


def kernel(
    phases, nx, tokens, act, prm, blk, out,
    own, act_z, prm_z, halo, halo_z, mate, pair_z, both,
    raw_o, raw_z, inv_o, inv_z, par_o, par_z, uu_o, uu_z, qf_o, qf_z,
    first_rates, filt, av, wv, ob, sb, rb, pf, pb, cb, rt, rx,
    load_sem, halo_sem, mate_sem, pair_sem, prm_sem, act_sem, halo_z_sem, inv_z_sem,
    fy_sem, fx_sem, fs_sem, py_sem, px_sem, swap_sem,
    row_sem, tot_sem, car_sem, z_sem, store_sem,
):
    nyc = ROWS * CORES
    ctx = nx * nyc
    groups = nx * ROWS
    channels = groups * LANES
    halves = 2
    per = nx // halves
    near = NEAR * per
    few = MODES // CORES
    wide = ROWS * LANES
    phase = lax.axis_index("phase")
    me = lax.axis_index("ctx")
    x = me // nyc
    yc = lax.rem(me, nyc)
    y = yc // CORES
    c = lax.rem(yc, CORES)
    after = lax.rem(me + 1, ctx)
    before = lax.rem(me + ctx - 1, ctx)
    twin = x * nyc + y * CORES + (1 - c)
    above = lax.rem(phase + 1, phases)
    below = lax.rem(phase + phases - 1, phases)
    far = pl.ds(near * wide, channels - near * wide)

    load = pltpu.make_async_copy(act, own, load_sem)
    load.start()
    barrier = pltpu.get_barrier_semaphore()

    def greet(where):
        pl.semaphore_signal(barrier, inc=1, device_id=where, device_id_type=MESH)

    def greet_row(p, carry):
        greet({"ctx": x * nyc + lax.rem(yc + p, nyc)})
        return carry

    lax.fori_loop(1, nyc, greet_row, 0)

    def greet_col(p, carry):
        greet({"ctx": lax.rem(x + p, nx) * nyc + yc})
        return carry

    lax.fori_loop(1, nx, greet_col, 0)

    def greet_below(p, carry):
        greet({"phase": below, "ctx": x * nyc + p})
        return carry

    lax.fori_loop(0, nyc, greet_below, 0)
    greet({"ctx": before})
    greet({"phase": below, "ctx": before})

    def channel_rows(tile_ref, dest, g):
        tile = tile_ref[:, g * LANES:(g + 1) * LANES].astype(F32)
        dest[pl.ds(g, 8, stride=groups), :] = tile[:8]
        dest[pl.ds(8 * groups + g, 8, stride=groups), :] = tile[8:]

    for g in range(groups):
        channel_rows(prm, par_o, g)

    def place(dest, tile, at, g):
        dest[pl.ds(at * groups + g, 8, stride=groups), :] = tile[:8]
        dest[pl.ds((at + 8) * groups + g, 8, stride=groups), :] = tile[8:]

    def spread(tile_ref, source, at):
        total = jnp.zeros((16, LANES), F32)
        for g in range(groups):
            tile = tile_ref[pl.ds(source, 16), g * LANES:(g + 1) * LANES].astype(F32)
            place(raw_o, tile, at, g)
            total = total + tile * tile
        mean = jnp.sum(total, axis=1, keepdims=True) * (1.0 / channels)
        inv_o[pl.ds(at, 16), :] = jnp.broadcast_to(lax.rsqrt(mean + 1e-06), (16, LANES))

    def spread_own(i, carry):
        start = pl.multiple_of(i * 16, 16)
        spread(own, start, start + 16)
        return carry

    load.wait()
    lax.fori_loop(0, tokens // 16, spread_own, 0)

    pl.semaphore_wait(barrier, nyc - 1 + nx - 1 + nyc + 2)

    def send(src, dst, sems, where):
        pltpu.make_async_remote_copy(
            src_ref=src, dst_ref=dst, send_sem=sems.at[0], recv_sem=sems.at[1],
            device_id=where, device_id_type=MESH,
        ).start()

    def slot_of(j):
        return pl.ds(pl.multiple_of(j * MODES, MODES), MODES)

    def few_of(j):
        return pl.ds(pl.multiple_of(j * few, few), few)

    def send_row(src, dst, sems, up):
        def one(p, carry):
            j = lax.rem(yc + p, nyc)
            where = {"phase": above, "ctx": x * nyc + j} if up else {"ctx": x * nyc + j}
            send(src.at[slot_of(j)], dst.at[slot_of(yc)], sems, where)
            return carry
        lax.fori_loop(0 if up else 1, nyc, one, 0)

    def send_col(src, dst, sems):
        def one(p, carry):
            send(src, dst, sems, {"ctx": lax.rem(x + p, nx) * nyc + yc})
            return carry
        lax.fori_loop(1, nx, one, 0)

    def send_line(src, dst, sems):
        def one(p, carry):
            send(src, dst, sems, {"ctx": x * nyc + lax.rem(y + p, ROWS) * CORES + c})
            return carry
        lax.fori_loop(1, ROWS, one, 0)

    def send_act(q, start, count):
        part = pl.ds(q * wide, wide)
        rows = pl.ds(start, count)
        send(act.at[rows, part], act_z.at[rows, part], act_sem.at[q], {"phase": above})

    def send_acts(point):
        for q, start, count in PLAN[point]:
            if q >= near:
                send_act(q, start, count)

    send(blk, mate, mate_sem, {"ctx": twin})
    send(act.at[pl.ds(tokens - 16, 16)], halo, halo_sem, {"ctx": after})
    group = x * ROWS + y
    drain(mate, mate_sem.at[1])
    both[...] = blk[...] + mate[...]
    first_rates[c, few_of(group), :] = both[few_of(c), :]
    send_line(first_rates.at[c, few_of(group)], first_rates.at[c, few_of(group)], fy_sem)
    send(both.at[slot_of(c)], pair_z, pair_sem, {"phase": above})
    send(act.at[pl.ds(tokens - 16, 16), far], halo_z.at[:, far], halo_z_sem,
         {"phase": above, "ctx": after})
    send(inv_o.at[pl.ds(tokens, 16)], inv_z.at[pl.ds(0, 16)], inv_z_sem.at[1],
         {"phase": above, "ctx": after})
    send_acts(0)

    drain(halo, halo_sem.at[1])
    spread(halo, 0, 0)

    def rows_of(token, q):
        return pl.ds(pl.multiple_of(token * groups + 8 * q, 8), 8)

    def fixed(r, q):
        return slice(r * groups + 8 * q, r * groups + 8 * q + 8)

    first = jnp.where(me > 0, 1.0, 0.0).astype(F32)

    def features(q, raw, scale, par, uu, qf):
        gain = par[fixed(0, q), :]
        taps = [par[fixed(1 + j, q), :] for j in range(9)]

        def normed(token):
            value = raw[rows_of(token, q), :] * scale[pl.ds(token, 1), :] * gain
            return value.astype(BF16).astype(F32)

        def one(i, carry):
            back1, back2 = carry
            for k in range(4):
                t = i * 4 + k
                now = normed(t + 16)
                feats = [
                    None if b == 0 and qf is None else
                    (taps[3 * b] * now + taps[3 * b + 1] * back1) + taps[3 * b + 2] * back2
                    for b in range(3)
                ]
                if qf is not None:
                    qf[rows_of(t, q), :] = feats[0]
                uu[rows_of(t, q), :] = (feats[1] * feats[2]).astype(BF16).astype(F32)
                back1, back2 = now, back1
            return back1, back2

        lax.fori_loop(0, tokens // 4, one, (normed(15) * first, normed(14) * first))

    def features_own(q):
        features(q, raw_o, inv_o, par_o, uu_o, qf_o if q < near else None)

    for q in range(per):
        features_own(q)

    drain(first_rates.at[0, pl.ds(0, (ROWS - 1) * few)], fy_sem.at[1])
    line = pl.ds(pl.multiple_of(x * ROWS * few, ROWS * few), ROWS * few)
    send_col(first_rates.at[c, line], first_rates.at[c, line], fx_sem)

    drain(pair_z, pair_sem.at[1])
    home = jnp.broadcast_to(jnp.where(x < near, 1.0, 0.0).astype(F32), (MODES, LANES))
    filt[c, slot_of(group), :] = jnp.where(home > 0.5, both[slot_of(c), :], pair_z[...])
    send_line(filt.at[c, slot_of(group)], filt.at[c, slot_of(group)], py_sem)
    send_acts(1)

    for q in range(per, nx):
        features_own(q)

    drain(first_rates.at[0, pl.ds(0, (nx - 1) * ROWS * few)], fx_sem.at[1])
    send(first_rates.at[c], first_rates.at[c], fs_sem, {"ctx": twin})
    drain(first_rates.at[0], fs_sem.at[1])

    def end_state(h):
        for k in range(per):
            q = per * h + k
            decay = [
                jnp.exp(-first_rates[
                    r // few, pl.ds(q * ROWS * few + r % few, 8, stride=few), :])
                for r in range(MODES)
            ]
            for r in range(MODES):
                av[fixed(r, q), :] = decay[r]
            decay = [av[fixed(r, q), :] for r in range(MODES)]

            def one(i, state):
                for step in range(4):
                    value = uu_o[rows_of(i * 4 + step, q), :]
                    state = tuple(decay[r] * state[r] + value for r in range(MODES))
                return state

            state = lax.fori_loop(
                0, tokens // 4, one, tuple(jnp.zeros((8, LANES), F32) for _ in range(MODES))
            )
            for r in range(MODES):
                sb[h, pl.ds(k * MODES + r, 8, stride=CORES * MODES), :] = state[r]
        send_row(sb.at[h], rb.at[h], row_sem.at[h], False)
        rb[h, slot_of(yc), :] = sb[h, slot_of(yc), :]

    def own_rate(h):
        at = few_of((per * h + c) * ROWS + y)
        return jnp.concatenate([first_rates[0, at, :], first_rates[1, at, :]], axis=0)

    def line_sum(h):
        drain(rb.at[h, pl.ds(0, (nyc - 1) * MODES)], row_sem.at[h, 1])
        shard_decay = jnp.exp(own_rate(h) * (-float(tokens)))
        state = jnp.zeros((MODES, LANES), F32)
        for j in range(nyc):
            pf[h, j * MODES:(j + 1) * MODES, :] = state
            state = shard_decay * state + rb[h, j * MODES:(j + 1) * MODES, :]
        rt[h] = state
        rx[h, slot_of(x), :] = state
        send_col(rt.at[h], rx.at[h, slot_of(x)], tot_sem.at[h])

    def carries(h):
        drain(rx.at[h, pl.ds(0, (nx - 1) * MODES)], tot_sem.at[h, 1])
        shard_decay = jnp.exp(own_rate(h) * (-float(tokens)))
        line_decay = jnp.exp(own_rate(h) * (-float(tokens * nyc)))
        enter = jnp.zeros((MODES, LANES), F32)
        for k in range(nx):
            earlier = jnp.broadcast_to(jnp.where(k < x, 1.0, 0.0).astype(F32), (MODES, LANES))
            longer = line_decay * enter + rx[h, k * MODES:(k + 1) * MODES, :]
            enter = jnp.where(earlier > 0.5, longer, enter)
        for j in range(nyc):
            pb[h, j * MODES:(j + 1) * MODES, :] = pf[h, j * MODES:(j + 1) * MODES, :] + enter
            enter = enter * shard_decay
        send_row(pb.at[h], cb.at[h], car_sem.at[h], h >= NEAR)
        if h < NEAR:
            cb[h, slot_of(yc), :] = pb[h, slot_of(yc), :]

    def car_slots(h):
        return cb.at[h, pl.ds(0, (nyc if h >= NEAR else nyc - 1) * MODES)]

    def features_far(q):
        drain(act_z.at[:, pl.ds(q * wide, wide)], act_sem.at[q, 1])

        def spread_other(i, carry):
            start = pl.multiple_of(i * 16, 16)
            for g in range(8 * q, 8 * q + 8):
                tile = act_z[pl.ds(start, 16), g * LANES:(g + 1) * LANES].astype(F32)
                place(raw_z, tile, start + 16, g)
            return carry

        lax.fori_loop(0, tokens // 16, spread_other, 0)
        for g in range(8 * q, 8 * q + 8):
            place(raw_z, halo_z[:, g * LANES:(g + 1) * LANES].astype(F32), 0, g)
        features(q, raw_z, inv_z, par_z, uu_z, qf_z)

    def aligned(q):
        for r in range(MODES):
            at = pl.ds(q * ROWS * MODES + r, 8, stride=MODES)
            av[fixed(r, q), :] = jnp.exp(-filt[0, at, :])
            wv[fixed(r, q), :] = filt[1, at, :]

    def finish(h, k):
        q = per * h + k
        raw, uu, qf, par = (
            (raw_o, uu_o, qf_o, par_o) if q < near else (raw_z, uu_z, qf_z, par_z))
        decay = [av[fixed(r, q), :] for r in range(MODES)]
        weight = [wv[fixed(r, q), :] for r in range(MODES)]
        skip = par[fixed(10, q), :]

        def one(i, state):
            for step in range(4):
                t = i * 4 + step
                value = uu[rows_of(t, q), :]
                state = tuple(decay[r] * state[r] + value for r in range(MODES))
                terms = [weight[r] * state[r] for r in range(MODES)]
                while len(terms) > 1:
                    terms = [terms[2 * m] + terms[2 * m + 1] for m in range(len(terms) // 2)]
                conv = terms[0].astype(BF16).astype(F32)
                qf[rows_of(t, q), :] = (
                    raw[rows_of(t + 16, q), :]
                    + qf[rows_of(t, q), :] * (conv + skip * value))
            return state

        state = tuple(
            cb[h, pl.ds(k * MODES + r, 8, stride=CORES * MODES), :] for r in range(MODES))
        lax.fori_loop(0, tokens // 4, one, state)

        def gather(i, carry):
            start = pl.multiple_of(i * 16, 16)
            for g in range(8 * q, 8 * q + 8):
                low = qf[pl.ds(start * groups + g, 8, stride=groups), :]
                high = qf[pl.ds((start + 8) * groups + g, 8, stride=groups), :]
                ob[pl.ds(start, 16), g * LANES:(g + 1) * LANES] = (
                    jnp.concatenate([low, high], axis=0).astype(BF16))
            return carry

        lax.fori_loop(0, tokens // 16, gather, 0)
        part = pl.ds(q * wide, wide)
        if q < near:
            send(ob.at[:, part], out.at[:, part], z_sem, {"phase": above})
        else:
            pltpu.make_async_copy(ob.at[:, part], out.at[:, part], store_sem).start()

    end_state(0)
    end_state(1)
    drain(filt.at[0, pl.ds(0, (ROWS - 1) * MODES)], py_sem.at[1])
    span = pl.ds(pl.multiple_of(x * ROWS * MODES, ROWS * MODES), ROWS * MODES)
    send_col(filt.at[c, span], filt.at[c, span], px_sem)
    send(prm.at[:, far], prm_z.at[:, far], prm_sem, {"phase": above})
    send(inv_o.at[pl.ds(16, tokens)], inv_z.at[pl.ds(16, tokens)], inv_z_sem.at[0],
         {"phase": above})
    send_acts(2)
    line_sum(0)
    line_sum(1)
    send_acts(3)
    drain(filt.at[0, pl.ds(0, (nx - 1) * ROWS * MODES)], px_sem.at[1])
    send(filt.at[c], filt.at[c], swap_sem, {"ctx": twin})
    carries(0)
    carries(1)
    send_acts(4)
    drain(filt.at[0], swap_sem.at[1])
    for q in range(nx):
        aligned(q)
    drain(prm_z.at[:, far], prm_sem.at[1])
    for g in range(near * ROWS, groups):
        channel_rows(prm_z, par_z, g)
    drain(halo_z.at[:, far], halo_z_sem.at[1])
    drain(inv_z.at[pl.ds(16, tokens)], inv_z_sem.at[0, 1])
    drain(inv_z.at[pl.ds(0, 16)], inv_z_sem.at[1, 1])
    if NEAR == 0:
        features_far(0)
        features_far(1)
        drain(car_slots(0), car_sem.at[0, 1])
        finish(0, 0)
        finish(0, 1)
        features_far(2)
        drain(car_slots(1), car_sem.at[1, 1])
        finish(1, 0)
        features_far(3)
        finish(1, 1)
    else:
        drain(car_slots(0), car_sem.at[0, 1])
        finish(0, 0)
        finish(0, 1)
        features_far(2)
        features_far(3)
        drain(car_slots(1), car_sem.at[1, 1])
        finish(1, 0)
        finish(1, 1)

    drain(blk, mate_sem.at[0])
    drain(pair_z, pair_sem.at[0])
    drain(halo, halo_sem.at[0])
    drain(prm_z.at[:, far], prm_sem.at[0])
    for q in range(near, nx):
        drain(act_z.at[:, pl.ds(q * wide, wide)], act_sem.at[q, 0])
    drain(halo_z.at[:, far], halo_z_sem.at[0])
    drain(inv_z.at[pl.ds(16, tokens)], inv_z_sem.at[0, 0])
    drain(inv_z.at[pl.ds(0, 16)], inv_z_sem.at[1, 0])
    drain(first_rates.at[0, pl.ds(0, (ROWS - 1) * few)], fy_sem.at[0])
    drain(first_rates.at[0, pl.ds(0, (nx - 1) * ROWS * few)], fx_sem.at[0])
    drain(first_rates.at[0], fs_sem.at[0])
    drain(filt.at[0, pl.ds(0, (ROWS - 1) * MODES)], py_sem.at[0])
    drain(filt.at[0, pl.ds(0, (nx - 1) * ROWS * MODES)], px_sem.at[0])
    drain(filt.at[0], swap_sem.at[0])
    for h in range(halves):
        drain(rb.at[h, pl.ds(0, (nyc - 1) * MODES)], row_sem.at[h, 0])
        drain(rx.at[h, pl.ds(0, (nx - 1) * MODES)], tot_sem.at[h, 0])
        drain(car_slots(h), car_sem.at[h, 0])
    drain(ob.at[:, far], store_sem)
    if NEAR:
        drain(ob.at[:, pl.ds(0, near * wide)], z_sem.at[0])
        drain(ob.at[:, pl.ds(0, near * wide)], z_sem.at[1])


def local(phases, nx, activations, norm_gain, short_taps, skip_gain, time_const, residues):
    act = activations[0]
    tokens, channels = act.shape
    groups = channels // LANES
    halves = 2
    nyc = ROWS * CORES
    prm = jnp.concatenate(
        [norm_gain, short_taps[0].reshape(9, channels), skip_gain,
         jnp.zeros((5, channels), BF16)], axis=0)
    rate = 1.0 / time_const[0]
    weight = residues[0] * jnp.sqrt(-jnp.expm1(-2.0 * rate))
    both = jnp.concatenate([rate.T, weight.T], axis=0)
    wide = jnp.concatenate([both, both], axis=1)
    half = LANES // CORES
    column = lax.broadcasted_iota(jnp.int32, wide.shape, 1) // half
    blk = jnp.where(column == lax.axis_index("ctx") % CORES, wide, 0.0)
    vmem = pltpu.VMEM
    dma = pltpu.SemaphoreType.DMA
    out = pl.pallas_call(
        functools.partial(kernel, phases, nx, tokens),
        out_shape=jax.ShapeDtypeStruct((tokens, channels), BF16),
        in_specs=[
            pl.BlockSpec(memory_space=pl.ANY),
            pl.BlockSpec(memory_space=vmem),
            pl.BlockSpec(memory_space=vmem),
        ],
        out_specs=pl.BlockSpec(memory_space=pl.ANY),
        scratch_shapes=[
            vmem((tokens, channels), BF16),
            vmem((tokens, channels), BF16),
            vmem((16, channels), BF16),
            vmem((16, channels), BF16),
            vmem((16, channels), BF16),
            vmem((2 * MODES, LANES), F32),
            vmem((MODES, LANES), F32),
            vmem((2 * MODES, LANES), F32),
            vmem(((tokens + 16) * groups, LANES), F32),
            vmem(((tokens + 16) * groups, LANES), F32),
            vmem((tokens + 16, LANES), F32),
            vmem((tokens + 16, LANES), F32),
            vmem((16 * groups, LANES), F32),
            vmem((16 * groups, LANES), F32),
            vmem((tokens * groups, LANES), F32),
            vmem((tokens * groups, LANES), F32),
            vmem((tokens * groups, LANES), F32),
            vmem((tokens * groups, LANES), F32),
            vmem((CORES, groups * MODES // CORES, LANES), F32),
            vmem((2, groups * MODES, LANES), F32),
            vmem((groups * MODES, LANES), F32),
            vmem((groups * MODES, LANES), F32),
            vmem((tokens, channels), BF16),
            vmem((halves, nyc * MODES, LANES), F32),
            vmem((halves, nyc * MODES, LANES), F32),
            vmem((halves, nyc * MODES, LANES), F32),
            vmem((halves, nyc * MODES, LANES), F32),
            vmem((halves, nyc * MODES, LANES), F32),
            vmem((halves, MODES, LANES), F32),
            vmem((halves, nx * MODES, LANES), F32),
            dma(()),
            dma((2,)),
            dma((2,)),
            dma((2,)),
            dma((2,)),
            dma((nx, 2)),
            dma((2,)),
            dma((2, 2)),
            dma((2,)),
            dma((2,)),
            dma((2,)),
            dma((2,)),
            dma((2,)),
            dma((2,)),
            dma((halves, 2)),
            dma((halves, 2)),
            dma((halves, 2)),
            dma((2,)),
            dma(()),
        ],
        compiler_params=pltpu.CompilerParams(
            collective_id=0, has_side_effects=True, vmem_limit_bytes=56 * 1024 * 1024),
    )(act, prm, blk)
    return out[None]


def solution(mesh):
    in_specs = (
        P("phase", "ctx", None),
        P("phase", None),
        P("phase", None, None, None),
        P("phase", None),
        P("phase", "ctx", None),
        P("phase", "ctx", None),
    )
    nx = mesh.shape["ctx"] // (ROWS * CORES)
    return jax.shard_map(
        functools.partial(local, mesh.shape["phase"], nx),
        mesh=mesh, in_specs=in_specs, out_specs=P("phase", "ctx", None), check_vma=False)
```

```python
import functools

import jax
import jax.numpy as jnp
from jax import lax
from jax.experimental import pallas as pl
from jax.experimental.pallas import tpu as pltpu
from jax.sharding import PartitionSpec as P

MESH = pl.DeviceIdType.MESH
LANES = 128
MODES = 16
ROWS = 8
CORES = 2
PARTS = ((0,), (1, 2, 3))
EARLY = 1
PLAN = (((1, 0, 128),), ((2, 0, 128),), ((3, 0, 128),), (), ())
KINDS = 11
F32 = jnp.float32
BF16 = jnp.bfloat16


def drain(ref, sem):
    pltpu.make_async_copy(ref, ref, sem).wait()


def kernel(
    phases, nx, tokens, act, gains, taps_in, skips, tau, res, out,
    blk, own, act_z, halo, halo_z, mate, pair_z, both,
    raw_o, raw_z, inv_o, inv_z, par_o, par_z, uu_o, uu_z, qf_o, qf_z,
    first_rates, filt, av, wv, ob, sb, rb, pf, pb, cb, rt, rx,
    load_sem, halo_sem, mate_sem, pair_sem, prm_sem, act_sem, halo_z_sem, inv_z_sem,
    fy_sem, fx_sem, fs_sem, py_sem, px_sem, swap_sem,
    row_sem, tot_sem, car_sem, z_sem, store_sem,
):
    nyc = ROWS * CORES
    ctx = nx * nyc
    groups = nx * ROWS
    channels = groups * LANES
    halves = 2
    near = len(PARTS[0])
    few = MODES // CORES
    wide = ROWS * LANES
    phase = lax.axis_index("phase")
    me = lax.axis_index("ctx")
    x = me // nyc
    yc = lax.rem(me, nyc)
    y = yc // CORES
    c = lax.rem(yc, CORES)
    after = lax.rem(me + 1, ctx)
    before = lax.rem(me + ctx - 1, ctx)
    twin = x * nyc + y * CORES + (1 - c)
    above = lax.rem(phase + 1, phases)
    below = lax.rem(phase + phases - 1, phases)
    far = pl.ds(near * wide, channels - near * wide)

    load = pltpu.make_async_copy(act, own, load_sem)
    load.start()
    barrier = pltpu.get_barrier_semaphore()

    def greet(where):
        pl.semaphore_signal(barrier, inc=1, device_id=where, device_id_type=MESH)

    def greet_row(p, carry):
        greet({"ctx": x * nyc + lax.rem(yc + p, nyc)})
        return carry

    lax.fori_loop(1, nyc, greet_row, 0)

    def greet_col(p, carry):
        greet({"ctx": lax.rem(x + p, nx) * nyc + yc})
        return carry

    lax.fori_loop(1, nx, greet_col, 0)

    def greet_below(p, carry):
        greet({"phase": below, "ctx": x * nyc + p})
        return carry

    lax.fori_loop(0, nyc, greet_below, 0)
    greet({"ctx": before})
    greet({"phase": below, "ctx": before})

    rates = 1.0 / tau[...]
    square = rates * rates
    sinh = rates * (1.0 + square / 6.0 * (1.0 + square / 20.0 * (1.0 + square / 42.0)))
    weights = res[...] * jnp.sqrt(2.0 * jnp.exp(-rates) * sinh)
    half = LANES // CORES
    for core in range(CORES):
        this = jnp.where(c == core, 1.0, 0.0).astype(F32)
        blk[0:MODES, core * half:(core + 1) * half] = rates * this
        blk[MODES:2 * MODES, core * half:(core + 1) * half] = weights * this

    for g in range(groups):
        lanes = slice(g * LANES, (g + 1) * LANES)
        base = g // 8 * KINDS * 8 + g % 8
        par_o[base:base + 1, :] = gains[:, lanes].astype(F32)
        for b in range(3):
            par_o[pl.ds(base + (1 + 3 * b) * 8, 3, stride=8), :] = taps_in[b, :, lanes].astype(F32)
        par_o[base + 80:base + 81, :] = skips[:, lanes].astype(F32)

    def place(dest, tile, at, g):
        dest[pl.ds(at * groups + g, 8, stride=groups), :] = tile[:8]
        dest[pl.ds((at + 8) * groups + g, 8, stride=groups), :] = tile[8:]

    def spread(tile_ref, source, at):
        total = jnp.zeros((16, LANES), F32)
        for g in range(groups):
            tile = tile_ref[pl.ds(source, 16), g * LANES:(g + 1) * LANES].astype(F32)
            place(raw_o, tile, at, g)
            total = total + tile * tile
        mean = jnp.sum(total, axis=1, keepdims=True) * (1.0 / channels)
        inv_o[pl.ds(at, 16), :] = jnp.broadcast_to(lax.rsqrt(mean + 1e-06), (16, LANES))

    def spread_own(i, carry):
        start = pl.multiple_of(i * 16, 16)
        spread(own, start, start + 16)
        return carry

    load.wait()
    lax.fori_loop(0, tokens // 16, spread_own, 0)

    pl.semaphore_wait(barrier, nyc - 1 + nx - 1 + nyc + 2)

    def send(src, dst, sems, where):
        pltpu.make_async_remote_copy(
            src_ref=src, dst_ref=dst, send_sem=sems.at[0], recv_sem=sems.at[1],
            device_id=where, device_id_type=MESH,
        ).start()

    def slot_of(j):
        return pl.ds(pl.multiple_of(j * MODES, MODES), MODES)

    def few_of(j):
        return pl.ds(pl.multiple_of(j * few, few), few)

    deep = [len(quarters) * few for quarters in PARTS]

    def deep_of(h, j):
        return pl.ds(pl.multiple_of(j * deep[h], few), deep[h])

    def send_row(h, src, dst, sems, up):
        def one(p, carry):
            j = lax.rem(yc + p, nyc)
            where = {"phase": above, "ctx": x * nyc + j} if up else {"ctx": x * nyc + j}
            send(src.at[deep_of(h, j)], dst.at[deep_of(h, yc)], sems, where)
            return carry
        lax.fori_loop(0 if up else 1, nyc, one, 0)

    def send_col(src, dst, sems):
        def one(p, carry):
            send(src, dst, sems, {"ctx": lax.rem(x + p, nx) * nyc + yc})
            return carry
        lax.fori_loop(1, nx, one, 0)

    def send_line(src, dst, sems):
        def one(p, carry):
            send(src, dst, sems, {"ctx": x * nyc + lax.rem(y + p, ROWS) * CORES + c})
            return carry
        lax.fori_loop(1, ROWS, one, 0)

    def send_act(q, start, count):
        part = pl.ds(q * wide, wide)
        rows = pl.ds(start, count)
        send(act.at[rows, part], act_z.at[rows, part], act_sem.at[q], {"phase": above})

    def send_acts(point):
        for q, start, count in PLAN[point]:
            if q >= near:
                send_act(q, start, count)

    send(blk, mate, mate_sem, {"ctx": twin})
    send(act.at[pl.ds(tokens - 16, 16)], halo, halo_sem, {"ctx": after})
    group = x * ROWS + y
    drain(mate, mate_sem.at[1])
    both[...] = blk[...] + mate[...]
    first_rates[c, few_of(group), :] = both[few_of(c), :]
    send_line(first_rates.at[c, few_of(group)], first_rates.at[c, few_of(group)], fy_sem)
    send(both.at[slot_of(c)], pair_z, pair_sem, {"phase": above})
    send(act.at[pl.ds(tokens - 16, 16), far], halo_z.at[:, far], halo_z_sem,
         {"phase": above, "ctx": after})
    send(inv_o.at[pl.ds(tokens, 16)], inv_z.at[pl.ds(0, 16)], inv_z_sem.at[1],
         {"phase": above, "ctx": after})
    send_acts(0)

    drain(halo, halo_sem.at[1])
    spread(halo, 0, 0)

    def rows_of(token, q):
        return pl.ds(pl.multiple_of(token * groups + 8 * q, 8), 8)

    def fixed(r, q):
        return slice(r * groups + 8 * q, r * groups + 8 * q + 8)

    def param(j, q):
        return slice((q * KINDS + j) * 8, (q * KINDS + j) * 8 + 8)

    far_par = pl.ds(near * KINDS * 8, (nx - near) * KINDS * 8)
    first = jnp.where(me > 0, 1.0, 0.0).astype(F32)

    def features(q, raw, scale, par, uu, qf):
        gain = par[param(0, q), :]
        taps = [par[param(1 + j, q), :] for j in range(9)]

        def normed(token):
            value = raw[rows_of(token, q), :] * scale[pl.ds(token, 1), :] * gain
            return value.astype(BF16).astype(F32)

        def one(i, carry):
            back1, back2 = carry
            for k in range(4):
                t = i * 4 + k
                now = normed(t + 16)
                feats = [
                    None if b == 0 and qf is None else
                    (taps[3 * b] * now + taps[3 * b + 1] * back1) + taps[3 * b + 2] * back2
                    for b in range(3)
                ]
                if qf is not None:
                    qf[rows_of(t, q), :] = feats[0]
                uu[rows_of(t, q), :] = (feats[1] * feats[2]).astype(BF16).astype(F32)
                back1, back2 = now, back1
            return back1, back2

        lax.fori_loop(0, tokens // 4, one, (normed(15) * first, normed(14) * first))

    def features_own(q):
        features(q, raw_o, inv_o, par_o, uu_o, qf_o if q < near else None)

    for q in PARTS[0]:
        features_own(q)

    drain(first_rates.at[0, pl.ds(0, (ROWS - 1) * few)], fy_sem.at[1])
    line = pl.ds(pl.multiple_of(x * ROWS * few, ROWS * few), ROWS * few)
    send_col(first_rates.at[c, line], first_rates.at[c, line], fx_sem)

    drain(pair_z, pair_sem.at[1])
    home = jnp.broadcast_to(jnp.where(x < near, 1.0, 0.0).astype(F32), (MODES, LANES))
    filt[c, slot_of(group), :] = jnp.where(home > 0.5, both[slot_of(c), :], pair_z[...])
    send_line(filt.at[c, slot_of(group)], filt.at[c, slot_of(group)], py_sem)
    send_acts(1)

    for q in PARTS[1]:
        features_own(q)

    drain(first_rates.at[0, pl.ds(0, (nx - 1) * ROWS * few)], fx_sem.at[1])
    send(first_rates.at[c], first_rates.at[c], fs_sem, {"ctx": twin})
    drain(first_rates.at[0], fs_sem.at[1])

    def strided(h, k, r):
        return pl.ds(r // few * deep[h] + k * few + r % few, 8, stride=CORES * deep[h])

    def end_state(h):
        for k, q in enumerate(PARTS[h]):
            decay = [
                jnp.exp(-first_rates[
                    r // few, pl.ds(q * ROWS * few + r % few, 8, stride=few), :])
                for r in range(MODES)
            ]
            for r in range(MODES):
                av[fixed(r, q), :] = decay[r]
            decay = [av[fixed(r, q), :] for r in range(MODES)]

            def one(i, state):
                for step in range(4):
                    value = uu_o[rows_of(i * 4 + step, q), :]
                    state = tuple(decay[r] * state[r] + value for r in range(MODES))
                return state

            state = lax.fori_loop(
                0, tokens // 4, one, tuple(jnp.zeros((8, LANES), F32) for _ in range(MODES))
            )
            for r in range(MODES):
                sb[h, strided(h, k, r), :] = state[r]
        send_row(h, sb.at[h], rb.at[h], row_sem.at[h], False)
        rb[h, deep_of(h, yc), :] = sb[h, deep_of(h, yc), :]

    def own_rate(h):
        return jnp.concatenate(
            [first_rates[c, few_of(q * ROWS + y), :] for q in PARTS[h]], axis=0)

    def line_sum(h):
        drain(rb.at[h, pl.ds(0, (nyc - 1) * deep[h])], row_sem.at[h, 1])
        shard_decay = jnp.exp(own_rate(h) * (-float(tokens)))
        state = jnp.zeros((deep[h], LANES), F32)
        for j in range(nyc):
            pf[h, j * deep[h]:(j + 1) * deep[h], :] = state
            state = shard_decay * state + rb[h, j * deep[h]:(j + 1) * deep[h], :]
        rt[h, 0:deep[h], :] = state
        rx[h, deep_of(h, x), :] = state
        send_col(rt.at[h, pl.ds(0, deep[h])], rx.at[h, deep_of(h, x)], tot_sem.at[h])

    def carries(h):
        drain(rx.at[h, pl.ds(0, (nx - 1) * deep[h])], tot_sem.at[h, 1])
        shard_decay = jnp.exp(own_rate(h) * (-float(tokens)))
        line_decay = jnp.exp(own_rate(h) * (-float(tokens * nyc)))
        enter = jnp.zeros((deep[h], LANES), F32)
        for k in range(nx):
            earlier = jnp.broadcast_to(jnp.where(k < x, 1.0, 0.0).astype(F32), (deep[h], LANES))
            longer = line_decay * enter + rx[h, k * deep[h]:(k + 1) * deep[h], :]
            enter = jnp.where(earlier > 0.5, longer, enter)
        for j in range(nyc):
            pb[h, j * deep[h]:(j + 1) * deep[h], :] = pf[h, j * deep[h]:(j + 1) * deep[h], :] + enter
            enter = enter * shard_decay
        send_row(h, pb.at[h], cb.at[h], car_sem.at[h], h > 0)
        if h == 0:
            cb[h, deep_of(h, yc), :] = pb[h, deep_of(h, yc), :]

    def car_slots(h):
        return cb.at[h, pl.ds(0, (nyc if h > 0 else nyc - 1) * deep[h])]

    def features_far(q):
        drain(act_z.at[:, pl.ds(q * wide, wide)], act_sem.at[q, 1])

        def spread_other(i, carry):
            start = pl.multiple_of(i * 16, 16)
            for g in range(8 * q, 8 * q + 8):
                tile = act_z[pl.ds(start, 16), g * LANES:(g + 1) * LANES].astype(F32)
                place(raw_z, tile, start + 16, g)
            return carry

        lax.fori_loop(0, tokens // 16, spread_other, 0)
        for g in range(8 * q, 8 * q + 8):
            place(raw_z, halo_z[:, g * LANES:(g + 1) * LANES].astype(F32), 0, g)
        features(q, raw_z, inv_z, par_z, uu_z, qf_z)

    def aligned(q):
        for r in range(MODES):
            at = pl.ds(q * ROWS * MODES + r, 8, stride=MODES)
            av[fixed(r, q), :] = jnp.exp(-filt[0, at, :])
            wv[fixed(r, q), :] = filt[1, at, :]

    def finish(h, k):
        q = PARTS[h][k]
        raw, uu, qf, par = (
            (raw_o, uu_o, qf_o, par_o) if q < near else (raw_z, uu_z, qf_z, par_z))
        decay = [av[fixed(r, q), :] for r in range(MODES)]
        weight = [wv[fixed(r, q), :] for r in range(MODES)]
        skip = par[param(10, q), :]

        def one(i, state):
            for step in range(4):
                t = i * 4 + step
                value = uu[rows_of(t, q), :]
                state = tuple(decay[r] * state[r] + value for r in range(MODES))
                terms = [weight[r] * state[r] for r in range(MODES)]
                while len(terms) > 1:
                    terms = [terms[2 * m] + terms[2 * m + 1] for m in range(len(terms) // 2)]
                conv = terms[0].astype(BF16).astype(F32)
                qf[rows_of(t, q), :] = (
                    raw[rows_of(t + 16, q), :]
                    + qf[rows_of(t, q), :] * (conv + skip * value))
            return state

        state = tuple(
            cb[h, strided(h, k, r), :] for r in range(MODES))
        lax.fori_loop(0, tokens // 4, one, state)

        def gather(i, carry):
            start = pl.multiple_of(i * 16, 16)
            for g in range(8 * q, 8 * q + 8):
                low = qf[pl.ds(start * groups + g, 8, stride=groups), :]
                high = qf[pl.ds((start + 8) * groups + g, 8, stride=groups), :]
                ob[pl.ds(start, 16), g * LANES:(g + 1) * LANES] = (
                    jnp.concatenate([low, high], axis=0).astype(BF16))
            return carry

        lax.fori_loop(0, tokens // 16, gather, 0)
        part = pl.ds(q * wide, wide)
        if q < near:
            send(ob.at[:, part], out.at[:, part], z_sem, {"phase": above})
        else:
            pltpu.make_async_copy(ob.at[:, part], out.at[:, part], store_sem).start()

    end_state(0)
    end_state(1)
    drain(filt.at[0, pl.ds(0, (ROWS - 1) * MODES)], py_sem.at[1])
    span = pl.ds(pl.multiple_of(x * ROWS * MODES, ROWS * MODES), ROWS * MODES)
    send_col(filt.at[c, span], filt.at[c, span], px_sem)
    send(par_o.at[far_par], par_z.at[far_par], prm_sem, {"phase": above})
    send(inv_o.at[pl.ds(16, tokens)], inv_z.at[pl.ds(16, tokens)], inv_z_sem.at[0],
         {"phase": above})
    send_acts(2)
    line_sum(0)
    line_sum(1)
    send_acts(3)
    drain(filt.at[0, pl.ds(0, (nx - 1) * ROWS * MODES)], px_sem.at[1])
    send(filt.at[c], filt.at[c], swap_sem, {"ctx": twin})
    carries(0)
    carries(1)
    send_acts(4)
    drain(filt.at[0], swap_sem.at[1])
    for q in range(nx):
        aligned(q)
    drain(par_z.at[far_par], prm_sem.at[1])
    drain(halo_z.at[:, far], halo_z_sem.at[1])
    drain(inv_z.at[pl.ds(16, tokens)], inv_z_sem.at[0, 1])
    drain(inv_z.at[pl.ds(0, 16)], inv_z_sem.at[1, 1])
    for q in PARTS[1][:EARLY]:
        features_far(q)
    drain(car_slots(0), car_sem.at[0, 1])
    for k in range(len(PARTS[0])):
        finish(0, k)
    for q in PARTS[1][EARLY:]:
        features_far(q)
    drain(car_slots(1), car_sem.at[1, 1])
    for k in range(len(PARTS[1])):
        finish(1, k)

    drain(blk, mate_sem.at[0])
    drain(pair_z, pair_sem.at[0])
    drain(halo, halo_sem.at[0])
    drain(par_z.at[far_par], prm_sem.at[0])
    for q in range(near, nx):
        drain(act_z.at[:, pl.ds(q * wide, wide)], act_sem.at[q, 0])
    drain(halo_z.at[:, far], halo_z_sem.at[0])
    drain(inv_z.at[pl.ds(16, tokens)], inv_z_sem.at[0, 0])
    drain(inv_z.at[pl.ds(0, 16)], inv_z_sem.at[1, 0])
    drain(first_rates.at[0, pl.ds(0, (ROWS - 1) * few)], fy_sem.at[0])
    drain(first_rates.at[0, pl.ds(0, (nx - 1) * ROWS * few)], fx_sem.at[0])
    drain(first_rates.at[0], fs_sem.at[0])
    drain(filt.at[0, pl.ds(0, (ROWS - 1) * MODES)], py_sem.at[0])
    drain(filt.at[0, pl.ds(0, (nx - 1) * ROWS * MODES)], px_sem.at[0])
    drain(filt.at[0], swap_sem.at[0])
    for h in range(halves):
        drain(rb.at[h, pl.ds(0, (nyc - 1) * deep[h])], row_sem.at[h, 0])
        drain(rx.at[h, pl.ds(0, (nx - 1) * deep[h])], tot_sem.at[h, 0])
        drain(car_slots(h), car_sem.at[h, 0])
    drain(ob.at[:, far], store_sem)
    drain(ob.at[:, pl.ds(0, near * wide)], z_sem.at[0])
    drain(ob.at[:, pl.ds(0, near * wide)], z_sem.at[1])


def local(phases, nx, activations, norm_gain, short_taps, skip_gain, time_const, residues):
    act = activations[0]
    tokens, channels = act.shape
    groups = channels // LANES
    halves = 2
    nyc = ROWS * CORES
    most = max(len(quarters) for quarters in PARTS) * MODES // CORES
    vmem = pltpu.VMEM
    dma = pltpu.SemaphoreType.DMA
    out = pl.pallas_call(
        functools.partial(kernel, phases, nx, tokens),
        out_shape=jax.ShapeDtypeStruct((tokens, channels), BF16),
        in_specs=[
            pl.BlockSpec(memory_space=pl.ANY),
            pl.BlockSpec(memory_space=vmem),
            pl.BlockSpec(memory_space=vmem),
            pl.BlockSpec(memory_space=vmem),
            pl.BlockSpec(memory_space=vmem),
            pl.BlockSpec(memory_space=vmem),
        ],
        out_specs=pl.BlockSpec(memory_space=pl.ANY),
        scratch_shapes=[
            vmem((2 * MODES, LANES), F32),
            vmem((tokens, channels), BF16),
            vmem((tokens, channels), BF16),
            vmem((16, channels), BF16),
            vmem((16, channels), BF16),
            vmem((2 * MODES, LANES), F32),
            vmem((MODES, LANES), F32),
            vmem((2 * MODES, LANES), F32),
            vmem(((tokens + 16) * groups, LANES), F32),
            vmem(((tokens + 16) * groups, LANES), F32),
            vmem((tokens + 16, LANES), F32),
            vmem((tokens + 16, LANES), F32),
            vmem((KINDS * groups, LANES), F32),
            vmem((KINDS * groups, LANES), F32),
            vmem((tokens * groups, LANES), F32),
            vmem((tokens * groups, LANES), F32),
            vmem((tokens * groups, LANES), F32),
            vmem((tokens * groups, LANES), F32),
            vmem((CORES, groups * MODES // CORES, LANES), F32),
            vmem((2, groups * MODES, LANES), F32),
            vmem((groups * MODES, LANES), F32),
            vmem((groups * MODES, LANES), F32),
            vmem((tokens, channels), BF16),
            vmem((halves, nyc * most, LANES), F32),
            vmem((halves, nyc * most, LANES), F32),
            vmem((halves, nyc * most, LANES), F32),
            vmem((halves, nyc * most, LANES), F32),
            vmem((halves, nyc * most, LANES), F32),
            vmem((halves, most, LANES), F32),
            vmem((halves, nx * most, LANES), F32),
            dma(()),
            dma((2,)),
            dma((2,)),
            dma((2,)),
            dma((2,)),
            dma((nx, 2)),
            dma((2,)),
            dma((2, 2)),
            dma((2,)),
            dma((2,)),
            dma((2,)),
            dma((2,)),
            dma((2,)),
            dma((2,)),
            dma((halves, 2)),
            dma((halves, 2)),
            dma((halves, 2)),
            dma((2,)),
            dma(()),
        ],
        compiler_params=pltpu.CompilerParams(
            collective_id=0, has_side_effects=True, vmem_limit_bytes=56 * 1024 * 1024),
    )(act, norm_gain, short_taps[0], skip_gain, time_const[0].T, residues[0].T)
    return out[None]


def solution(mesh):
    in_specs = (
        P("phase", "ctx", None),
        P("phase", None),
        P("phase", None, None, None),
        P("phase", None),
        P("phase", "ctx", None),
        P("phase", "ctx", None),
    )
    nx = mesh.shape["ctx"] // (ROWS * CORES)
    return jax.shard_map(
        functools.partial(local, mesh.shape["phase"], nx),
        mesh=mesh, in_specs=in_specs, out_specs=P("phase", "ctx", None), check_vma=False)
```

```python
import functools

import jax
import jax.numpy as jnp
from jax import lax
from jax.experimental import pallas as pl
from jax.experimental.pallas import tpu as pltpu
from jax.sharding import PartitionSpec as P

MESH = pl.DeviceIdType.MESH
LANES = 128
MODES = 16
ROWS = 8
CORES = 2
PARTS = ((0,), (1, 2, 3))
EARLY = 1
PLAN = (((1, 0, 128),), ((2, 0, 128),), ((3, 0, 128),), (), ())
KINDS = 11
F32 = jnp.float32
BF16 = jnp.bfloat16


def drain(ref, sem):
    pltpu.make_async_copy(ref, ref, sem).wait()


def kernel(
    phases, nx, tokens, act, gains, taps_in, skips, tau, res, out,
    blk, own, act_z, halo, halo_z, mate, pair_z, both,
    raw_o, raw_z, inv_o, inv_z, par_o, par_z, uu_o, uu_z, qf_o, qf_z,
    first_rates, filt, av, wv, ob, sb, rb, pf, pb, cb, rt, rx,
    load_sem, halo_sem, mate_sem, pair_sem, prm_sem, act_sem, halo_z_sem, inv_z_sem,
    fy_sem, fx_sem, fs_sem, py_sem, px_sem, swap_sem,
    row_sem, tot_sem, car_sem, z_sem, store_sem,
):
    nyc = ROWS * CORES
    ctx = nx * nyc
    groups = nx * ROWS
    channels = groups * LANES
    halves = 2
    near = len(PARTS[0])
    few = MODES // CORES
    wide = ROWS * LANES
    phase = lax.axis_index("phase")
    me = lax.axis_index("ctx")
    x = me // nyc
    yc = lax.rem(me, nyc)
    y = yc // CORES
    c = lax.rem(yc, CORES)
    after = lax.rem(me + 1, ctx)
    before = lax.rem(me + ctx - 1, ctx)
    twin = x * nyc + y * CORES + (1 - c)
    above = lax.rem(phase + 1, phases)
    below = lax.rem(phase + phases - 1, phases)
    far = pl.ds(near * wide, channels - near * wide)

    load = pltpu.make_async_copy(act, own, load_sem)
    load.start()
    barrier = pltpu.get_barrier_semaphore()

    def greet(where):
        pl.semaphore_signal(barrier, inc=1, device_id=where, device_id_type=MESH)

    def greet_row(p, carry):
        greet({"ctx": x * nyc + lax.rem(yc + p, nyc)})
        return carry

    lax.fori_loop(1, nyc, greet_row, 0)

    def greet_col(p, carry):
        greet({"ctx": lax.rem(x + p, nx) * nyc + yc})
        return carry

    lax.fori_loop(1, nx, greet_col, 0)

    def greet_below(p, carry):
        greet({"phase": below, "ctx": x * nyc + p})
        return carry

    lax.fori_loop(0, nyc, greet_below, 0)
    greet({"ctx": before})
    greet({"phase": below, "ctx": before})

    rates = 1.0 / tau[...]
    square = rates * rates
    sinh = rates * (1.0 + square / 6.0 * (1.0 + square / 20.0 * (1.0 + square / 42.0)))
    weights = res[...] * jnp.sqrt(2.0 * jnp.exp(-rates) * sinh)
    half = LANES // CORES
    for core in range(CORES):
        this = jnp.where(c == core, 1.0, 0.0).astype(F32)
        blk[0:MODES, core * half:(core + 1) * half] = rates * this
        blk[MODES:2 * MODES, core * half:(core + 1) * half] = weights * this

    for g in range(groups):
        lanes = slice(g * LANES, (g + 1) * LANES)
        base = g // 8 * KINDS * 8 + g % 8
        par_o[base:base + 1, :] = gains[:, lanes].astype(F32)
        for b in range(3):
            par_o[pl.ds(base + (1 + 3 * b) * 8, 3, stride=8), :] = taps_in[b, :, lanes].astype(F32)
        par_o[base + 80:base + 81, :] = skips[:, lanes].astype(F32)

    def place(dest, tile, at, g):
        dest[pl.ds(at * groups + g, 8, stride=groups), :] = tile[:8]
        dest[pl.ds((at + 8) * groups + g, 8, stride=groups), :] = tile[8:]

    def spread(tile_ref, source, at):
        total = jnp.zeros((16, LANES), F32)
        for g in range(groups):
            tile = tile_ref[pl.ds(source, 16), g * LANES:(g + 1) * LANES].astype(F32)
            place(raw_o, tile, at, g)
            total = total + tile * tile
        mean = jnp.sum(total, axis=1, keepdims=True) * (1.0 / channels)
        inv_o[pl.ds(at, 16), :] = jnp.broadcast_to(lax.rsqrt(mean + 1e-06), (16, LANES))

    def spread_own(i, carry):
        start = pl.multiple_of(i * 16, 16)
        spread(own, start, start + 16)
        return carry

    load.wait()
    lax.fori_loop(0, tokens // 16, spread_own, 0)

    pl.semaphore_wait(barrier, nyc - 1 + nx - 1 + nyc + 2)

    def send(src, dst, sems, where):
        pltpu.make_async_remote_copy(
            src_ref=src, dst_ref=dst, send_sem=sems.at[0], recv_sem=sems.at[1],
            device_id=where, device_id_type=MESH,
        ).start()

    def slot_of(j):
        return pl.ds(pl.multiple_of(j * MODES, MODES), MODES)

    def few_of(j):
        return pl.ds(pl.multiple_of(j * few, few), few)

    deep = [len(quarters) * few for quarters in PARTS]

    def deep_of(h, j):
        return pl.ds(pl.multiple_of(j * deep[h], few), deep[h])

    def far_first(k, count):
        return count // 2 + (1 - 2 * lax.rem(k, 2)) * (k // 2)

    def send_row(h, src, dst, sems, up):
        def one(p, carry):
            j = lax.rem(yc + far_first(p, nyc), nyc)
            where = {"phase": above, "ctx": x * nyc + j} if up else {"ctx": x * nyc + j}
            send(src.at[deep_of(h, j)], dst.at[deep_of(h, yc)], sems, where)
            return carry
        lax.fori_loop(1, nyc + 1 if up else nyc, one, 0, unroll=True)

    def send_col(src, dst, sems):
        def one(p, carry):
            send(src, dst, sems, {"ctx": lax.rem(x + far_first(p, nx), nx) * nyc + yc})
            return carry
        lax.fori_loop(1, nx, one, 0)

    def send_line(src, dst, sems):
        def one(p, carry):
            send(src, dst, sems, {"ctx": x * nyc + lax.rem(y + far_first(p, ROWS), ROWS) * CORES + c})
            return carry
        lax.fori_loop(1, ROWS, one, 0)

    def send_act(q, start, count):
        part = pl.ds(q * wide, wide)
        rows = pl.ds(start, count)
        send(act.at[rows, part], act_z.at[rows, part], act_sem.at[q], {"phase": above})

    def send_acts(point):
        for q, start, count in PLAN[point]:
            if q >= near:
                send_act(q, start, count)

    send(blk, mate, mate_sem, {"ctx": twin})
    group = x * ROWS + y
    drain(mate, mate_sem.at[1])
    both[...] = blk[...] + mate[...]
    first_rates[c, few_of(group), :] = both[few_of(c), :]
    send_line(first_rates.at[c, few_of(group)], first_rates.at[c, few_of(group)], fy_sem)
    send(act.at[pl.ds(tokens - 16, 16)], halo, halo_sem, {"ctx": after})
    send(both.at[slot_of(c)], pair_z, pair_sem, {"phase": above})
    send(act.at[pl.ds(tokens - 16, 16), far], halo_z.at[:, far], halo_z_sem,
         {"phase": above, "ctx": after})
    send(inv_o.at[pl.ds(tokens, 16)], inv_z.at[pl.ds(0, 16)], inv_z_sem.at[1],
         {"phase": above, "ctx": after})
    send_acts(0)

    drain(halo, halo_sem.at[1])
    spread(halo, 0, 0)

    def rows_of(token, q):
        return pl.ds(pl.multiple_of(token * groups + 8 * q, 8), 8)

    def fixed(r, q):
        return slice(r * groups + 8 * q, r * groups + 8 * q + 8)

    def param(j, q):
        return slice((q * KINDS + j) * 8, (q * KINDS + j) * 8 + 8)

    far_par = pl.ds(near * KINDS * 8, (nx - near) * KINDS * 8)
    first = jnp.where(me > 0, 1.0, 0.0).astype(F32)

    def features(q, raw, scale, par, uu, qf):
        gain = par[param(0, q), :]
        taps = [par[param(1 + j, q), :] for j in range(9)]

        def normed(token):
            value = raw[rows_of(token, q), :] * scale[pl.ds(token, 1), :] * gain
            return value.astype(BF16).astype(F32)

        def one(i, carry):
            back1, back2 = carry
            for k in range(4):
                t = i * 4 + k
                now = normed(t + 16)
                feats = [
                    None if b == 0 and qf is None else
                    (taps[3 * b] * now + taps[3 * b + 1] * back1) + taps[3 * b + 2] * back2
                    for b in range(3)
                ]
                if qf is not None:
                    qf[rows_of(t, q), :] = feats[0]
                uu[rows_of(t, q), :] = (feats[1] * feats[2]).astype(BF16).astype(F32)
                back1, back2 = now, back1
            return back1, back2

        lax.fori_loop(0, tokens // 4, one, (normed(15) * first, normed(14) * first))

    def features_own(q):
        features(q, raw_o, inv_o, par_o, uu_o, qf_o if q < near else None)

    for q in PARTS[0]:
        features_own(q)

    drain(first_rates.at[0, pl.ds(0, (ROWS - 1) * few)], fy_sem.at[1])
    line = pl.ds(pl.multiple_of(x * ROWS * few, ROWS * few), ROWS * few)
    send_col(first_rates.at[c, line], first_rates.at[c, line], fx_sem)

    drain(pair_z, pair_sem.at[1])
    home = jnp.broadcast_to(jnp.where(x < near, 1.0, 0.0).astype(F32), (MODES, LANES))
    filt[c, slot_of(group), :] = jnp.where(home > 0.5, both[slot_of(c), :], pair_z[...])
    send_line(filt.at[c, slot_of(group)], filt.at[c, slot_of(group)], py_sem)
    send_acts(1)

    for q in PARTS[1]:
        features_own(q)

    drain(first_rates.at[0, pl.ds(0, (nx - 1) * ROWS * few)], fx_sem.at[1])
    send(first_rates.at[c], first_rates.at[c], fs_sem, {"ctx": twin})
    drain(first_rates.at[0], fs_sem.at[1])

    def strided(h, k, r):
        return pl.ds(r // few * deep[h] + k * few + r % few, 8, stride=CORES * deep[h])

    def end_state(h):
        for k, q in enumerate(PARTS[h]):
            decay = [
                jnp.exp(-first_rates[
                    r // few, pl.ds(q * ROWS * few + r % few, 8, stride=few), :])
                for r in range(MODES)
            ]
            for r in range(MODES):
                av[fixed(r, q), :] = decay[r]
            decay = [av[fixed(r, q), :] for r in range(MODES)]

            def one(i, state):
                for step in range(4):
                    value = uu_o[rows_of(i * 4 + step, q), :]
                    state = tuple(decay[r] * state[r] + value for r in range(MODES))
                return state

            state = lax.fori_loop(
                0, tokens // 4, one, tuple(jnp.zeros((8, LANES), F32) for _ in range(MODES))
            )
            for r in range(MODES):
                sb[h, strided(h, k, r), :] = state[r]
        send_row(h, sb.at[h], rb.at[h], row_sem.at[h], False)
        rb[h, deep_of(h, yc), :] = sb[h, deep_of(h, yc), :]

    def own_rate(h):
        return jnp.concatenate(
            [first_rates[c, few_of(q * ROWS + y), :] for q in PARTS[h]], axis=0)

    def line_sum(h):
        drain(rb.at[h, pl.ds(0, (nyc - 1) * deep[h])], row_sem.at[h, 1])
        shard_decay = jnp.exp(own_rate(h) * (-float(tokens)))
        state = jnp.zeros((deep[h], LANES), F32)
        for j in range(nyc):
            pf[h, j * deep[h]:(j + 1) * deep[h], :] = state
            state = shard_decay * state + rb[h, j * deep[h]:(j + 1) * deep[h], :]
        rt[h, 0:deep[h], :] = state
        rx[h, deep_of(h, x), :] = state
        send_col(rt.at[h, pl.ds(0, deep[h])], rx.at[h, deep_of(h, x)], tot_sem.at[h])

    def carries(h):
        drain(rx.at[h, pl.ds(0, (nx - 1) * deep[h])], tot_sem.at[h, 1])
        shard_decay = jnp.exp(own_rate(h) * (-float(tokens)))
        line_decay = jnp.exp(own_rate(h) * (-float(tokens * nyc)))
        enter = jnp.zeros((deep[h], LANES), F32)
        for k in range(nx):
            earlier = jnp.broadcast_to(jnp.where(k < x, 1.0, 0.0).astype(F32), (deep[h], LANES))
            longer = line_decay * enter + rx[h, k * deep[h]:(k + 1) * deep[h], :]
            enter = jnp.where(earlier > 0.5, longer, enter)
        for j in range(nyc):
            pb[h, j * deep[h]:(j + 1) * deep[h], :] = pf[h, j * deep[h]:(j + 1) * deep[h], :] + enter
            enter = enter * shard_decay
        send_row(h, pb.at[h], cb.at[h], car_sem.at[h], h > 0)
        if h == 0:
            cb[h, deep_of(h, yc), :] = pb[h, deep_of(h, yc), :]

    def car_slots(h):
        return cb.at[h, pl.ds(0, (nyc if h > 0 else nyc - 1) * deep[h])]

    def features_far(q):
        drain(act_z.at[:, pl.ds(q * wide, wide)], act_sem.at[q, 1])

        def spread_other(i, carry):
            start = pl.multiple_of(i * 16, 16)
            for g in range(8 * q, 8 * q + 8):
                tile = act_z[pl.ds(start, 16), g * LANES:(g + 1) * LANES].astype(F32)
                place(raw_z, tile, start + 16, g)
            return carry

        lax.fori_loop(0, tokens // 16, spread_other, 0)
        for g in range(8 * q, 8 * q + 8):
            place(raw_z, halo_z[:, g * LANES:(g + 1) * LANES].astype(F32), 0, g)
        features(q, raw_z, inv_z, par_z, uu_z, qf_z)

    def aligned(q):
        for r in range(MODES):
            at = pl.ds(q * ROWS * MODES + r, 8, stride=MODES)
            av[fixed(r, q), :] = jnp.exp(-filt[0, at, :])
            wv[fixed(r, q), :] = filt[1, at, :]

    def finish(h, k):
        q = PARTS[h][k]
        raw, uu, qf, par = (
            (raw_o, uu_o, qf_o, par_o) if q < near else (raw_z, uu_z, qf_z, par_z))
        decay = [av[fixed(r, q), :] for r in range(MODES)]
        weight = [wv[fixed(r, q), :] for r in range(MODES)]
        skip = par[param(10, q), :]

        def one(i, state):
            for step in range(4):
                t = i * 4 + step
                value = uu[rows_of(t, q), :]
                state = tuple(decay[r] * state[r] + value for r in range(MODES))
                terms = [weight[r] * state[r] for r in range(MODES)]
                while len(terms) > 1:
                    terms = [terms[2 * m] + terms[2 * m + 1] for m in range(len(terms) // 2)]
                conv = terms[0].astype(BF16).astype(F32)
                qf[rows_of(t, q), :] = (
                    raw[rows_of(t + 16, q), :]
                    + qf[rows_of(t, q), :] * (conv + skip * value))
            return state

        state = tuple(
            cb[h, strided(h, k, r), :] for r in range(MODES))
        lax.fori_loop(0, tokens // 4, one, state)

        def gather(i, carry):
            start = pl.multiple_of(i * 16, 16)
            for g in range(8 * q, 8 * q + 8):
                low = qf[pl.ds(start * groups + g, 8, stride=groups), :]
                high = qf[pl.ds((start + 8) * groups + g, 8, stride=groups), :]
                ob[pl.ds(start, 16), g * LANES:(g + 1) * LANES] = (
                    jnp.concatenate([low, high], axis=0).astype(BF16))
            return carry

        lax.fori_loop(0, tokens // 16, gather, 0)
        part = pl.ds(q * wide, wide)
        if q < near:
            send(ob.at[:, part], out.at[:, part], z_sem, {"phase": above})
        else:
            pltpu.make_async_copy(ob.at[:, part], out.at[:, part], store_sem).start()

    end_state(0)
    end_state(1)
    drain(filt.at[0, pl.ds(0, (ROWS - 1) * MODES)], py_sem.at[1])
    span = pl.ds(pl.multiple_of(x * ROWS * MODES, ROWS * MODES), ROWS * MODES)
    send_col(filt.at[c, span], filt.at[c, span], px_sem)
    send(par_o.at[far_par], par_z.at[far_par], prm_sem, {"phase": above})
    send(inv_o.at[pl.ds(16, tokens)], inv_z.at[pl.ds(16, tokens)], inv_z_sem.at[0],
         {"phase": above})
    send_acts(2)
    line_sum(0)
    line_sum(1)
    send_acts(3)
    carries(0)
    drain(filt.at[0, pl.ds(0, (nx - 1) * ROWS * MODES)], px_sem.at[1])
    send(filt.at[c], filt.at[c], swap_sem, {"ctx": twin})
    carries(1)
    send_acts(4)
    drain(filt.at[0], swap_sem.at[1])
    for q in range(nx):
        aligned(q)
    drain(par_z.at[far_par], prm_sem.at[1])
    drain(halo_z.at[:, far], halo_z_sem.at[1])
    drain(inv_z.at[pl.ds(16, tokens)], inv_z_sem.at[0, 1])
    drain(inv_z.at[pl.ds(0, 16)], inv_z_sem.at[1, 1])
    for q in PARTS[1][:EARLY]:
        features_far(q)
    drain(car_slots(0), car_sem.at[0, 1])
    for k in range(len(PARTS[0])):
        finish(0, k)
    for q in PARTS[1][EARLY:]:
        features_far(q)
    drain(car_slots(1), car_sem.at[1, 1])
    for k in range(len(PARTS[1])):
        finish(1, k)

    drain(blk, mate_sem.at[0])
    drain(pair_z, pair_sem.at[0])
    drain(halo, halo_sem.at[0])
    drain(par_z.at[far_par], prm_sem.at[0])
    for q in range(near, nx):
        drain(act_z.at[:, pl.ds(q * wide, wide)], act_sem.at[q, 0])
    drain(halo_z.at[:, far], halo_z_sem.at[0])
    drain(inv_z.at[pl.ds(16, tokens)], inv_z_sem.at[0, 0])
    drain(inv_z.at[pl.ds(0, 16)], inv_z_sem.at[1, 0])
    drain(first_rates.at[0, pl.ds(0, (ROWS - 1) * few)], fy_sem.at[0])
    drain(first_rates.at[0, pl.ds(0, (nx - 1) * ROWS * few)], fx_sem.at[0])
    drain(first_rates.at[0], fs_sem.at[0])
    drain(filt.at[0, pl.ds(0, (ROWS - 1) * MODES)], py_sem.at[0])
    drain(filt.at[0, pl.ds(0, (nx - 1) * ROWS * MODES)], px_sem.at[0])
    drain(filt.at[0], swap_sem.at[0])
    for h in range(halves):
        drain(rb.at[h, pl.ds(0, (nyc - 1) * deep[h])], row_sem.at[h, 0])
        drain(rx.at[h, pl.ds(0, (nx - 1) * deep[h])], tot_sem.at[h, 0])
        drain(car_slots(h), car_sem.at[h, 0])
    drain(ob.at[:, far], store_sem)
    drain(ob.at[:, pl.ds(0, near * wide)], z_sem.at[0])
    drain(ob.at[:, pl.ds(0, near * wide)], z_sem.at[1])


def local(phases, nx, activations, norm_gain, short_taps, skip_gain, time_const, residues):
    act = activations[0]
    tokens, channels = act.shape
    groups = channels // LANES
    halves = 2
    nyc = ROWS * CORES
    most = max(len(quarters) for quarters in PARTS) * MODES // CORES
    vmem = pltpu.VMEM
    dma = pltpu.SemaphoreType.DMA
    out = pl.pallas_call(
        functools.partial(kernel, phases, nx, tokens),
        out_shape=jax.ShapeDtypeStruct((tokens, channels), BF16),
        in_specs=[
            pl.BlockSpec(memory_space=pl.ANY),
            pl.BlockSpec(memory_space=vmem),
            pl.BlockSpec(memory_space=vmem),
            pl.BlockSpec(memory_space=vmem),
            pl.BlockSpec(memory_space=vmem),
            pl.BlockSpec(memory_space=vmem),
        ],
        out_specs=pl.BlockSpec(memory_space=pl.ANY),
        scratch_shapes=[
            vmem((2 * MODES, LANES), F32),
            vmem((tokens, channels), BF16),
            vmem((tokens, channels), BF16),
            vmem((16, channels), BF16),
            vmem((16, channels), BF16),
            vmem((2 * MODES, LANES), F32),
            vmem((MODES, LANES), F32),
            vmem((2 * MODES, LANES), F32),
            vmem(((tokens + 16) * groups, LANES), F32),
            vmem(((tokens + 16) * groups, LANES), F32),
            vmem((tokens + 16, LANES), F32),
            vmem((tokens + 16, LANES), F32),
            vmem((KINDS * groups, LANES), F32),
            vmem((KINDS * groups, LANES), F32),
            vmem((tokens * groups, LANES), F32),
            vmem((tokens * groups, LANES), F32),
            vmem((tokens * groups, LANES), F32),
            vmem((tokens * groups, LANES), F32),
            vmem((CORES, groups * MODES // CORES, LANES), F32),
            vmem((2, groups * MODES, LANES), F32),
            vmem((groups * MODES, LANES), F32),
            vmem((groups * MODES, LANES), F32),
            vmem((tokens, channels), BF16),
            vmem((halves, nyc * most, LANES), F32),
            vmem((halves, nyc * most, LANES), F32),
            vmem((halves, nyc * most, LANES), F32),
            vmem((halves, nyc * most, LANES), F32),
            vmem((halves, nyc * most, LANES), F32),
            vmem((halves, most, LANES), F32),
            vmem((halves, nx * most, LANES), F32),
            dma(()),
            dma((2,)),
            dma((2,)),
            dma((2,)),
            dma((2,)),
            dma((nx, 2)),
            dma((2,)),
            dma((2, 2)),
            dma((2,)),
            dma((2,)),
            dma((2,)),
            dma((2,)),
            dma((2,)),
            dma((2,)),
            dma((halves, 2)),
            dma((halves, 2)),
            dma((halves, 2)),
            dma((2,)),
            dma(()),
        ],
        compiler_params=pltpu.CompilerParams(
            collective_id=0, has_side_effects=True, vmem_limit_bytes=56 * 1024 * 1024),
    )(act, norm_gain, short_taps[0], skip_gain, time_const[0].T, residues[0].T)
    return out[None]


def solution(mesh):
    in_specs = (
        P("phase", "ctx", None),
        P("phase", None),
        P("phase", None, None, None),
        P("phase", None),
        P("phase", "ctx", None),
        P("phase", "ctx", None),
    )
    nx = mesh.shape["ctx"] // (ROWS * CORES)
    return jax.shard_map(
        functools.partial(local, mesh.shape["phase"], nx),
        mesh=mesh, in_specs=in_specs, out_specs=P("phase", "ctx", None), check_vma=False)
```

```python
import functools

import jax
import jax.numpy as jnp
from jax import lax
from jax.experimental import pallas as pl
from jax.experimental.pallas import tpu as pltpu
from jax.sharding import PartitionSpec as P

MESH = pl.DeviceIdType.MESH
LANES = 128
MODES = 16
ROWS = 8
CORES = 2
PARTS = ((0,), (1, 2, 3))
EARLY = 1
PLAN = (((1, 0, 128),), ((2, 0, 128),), ((3, 0, 128),), (), ())
CUTS = 2
KINDS = 11
F32 = jnp.float32
BF16 = jnp.bfloat16


def drain(ref, sem):
    pltpu.make_async_copy(ref, ref, sem).wait()


def kernel(
    phases, nx, tokens, act, gains, taps_in, skips, tau, res, out,
    blk, own, act_z, halo, halo_z, mate, pair_z, both,
    raw_o, raw_z, inv_o, inv_z, par_o, par_z, uu_o, uu_z, qf_o, qf_z,
    first_rates, filt, av, wv, ob, sb, rb, pf, pb, cb, rt, rx,
    load_sem, halo_sem, mate_sem, pair_sem, prm_sem, act_sem, halo_z_sem, inv_z_sem,
    fy_sem, fx_sem, fs_sem, py_sem, px_sem, swap_sem,
    row_sem, tot_sem, car_sem, z_sem, store_sem,
):
    nyc = ROWS * CORES
    ctx = nx * nyc
    groups = nx * ROWS
    channels = groups * LANES
    halves = 2
    near = len(PARTS[0])
    few = MODES // CORES
    wide = ROWS * LANES
    phase = lax.axis_index("phase")
    me = lax.axis_index("ctx")
    x = me // nyc
    yc = lax.rem(me, nyc)
    y = yc // CORES
    c = lax.rem(yc, CORES)
    after = lax.rem(me + 1, ctx)
    before = lax.rem(me + ctx - 1, ctx)
    twin = x * nyc + y * CORES + (1 - c)
    above = lax.rem(phase + 1, phases)
    below = lax.rem(phase + phases - 1, phases)
    far = pl.ds(near * wide, channels - near * wide)

    load = pltpu.make_async_copy(act, own, load_sem)
    load.start()
    barrier = pltpu.get_barrier_semaphore()

    def greet(where):
        pl.semaphore_signal(barrier, inc=1, device_id=where, device_id_type=MESH)

    def greet_row(p, carry):
        greet({"ctx": x * nyc + lax.rem(yc + p, nyc)})
        return carry

    lax.fori_loop(1, nyc, greet_row, 0)

    def greet_col(p, carry):
        greet({"ctx": lax.rem(x + p, nx) * nyc + yc})
        return carry

    lax.fori_loop(1, nx, greet_col, 0)

    def greet_below(p, carry):
        greet({"phase": below, "ctx": x * nyc + p})
        return carry

    lax.fori_loop(0, nyc, greet_below, 0)
    greet({"ctx": before})
    greet({"phase": below, "ctx": before})

    rates = 1.0 / tau[...]
    square = rates * rates
    sinh = rates * (1.0 + square / 6.0 * (1.0 + square / 20.0 * (1.0 + square / 42.0)))
    weights = res[...] * jnp.sqrt(2.0 * jnp.exp(-rates) * sinh)
    half = LANES // CORES
    for core in range(CORES):
        this = jnp.where(c == core, 1.0, 0.0).astype(F32)
        blk[0:MODES, core * half:(core + 1) * half] = rates * this
        blk[MODES:2 * MODES, core * half:(core + 1) * half] = weights * this

    for g in range(groups):
        lanes = slice(g * LANES, (g + 1) * LANES)
        base = g // 8 * KINDS * 8 + g % 8
        par_o[base:base + 1, :] = gains[:, lanes].astype(F32)
        for b in range(3):
            par_o[pl.ds(base + (1 + 3 * b) * 8, 3, stride=8), :] = taps_in[b, :, lanes].astype(F32)
        par_o[base + 80:base + 81, :] = skips[:, lanes].astype(F32)

    def place(dest, tile, at, g):
        dest[pl.ds(at * groups + g, 8, stride=groups), :] = tile[:8]
        dest[pl.ds((at + 8) * groups + g, 8, stride=groups), :] = tile[8:]

    def spread(tile_ref, source, at):
        total = jnp.zeros((16, LANES), F32)
        for g in range(groups):
            tile = tile_ref[pl.ds(source, 16), g * LANES:(g + 1) * LANES].astype(F32)
            place(raw_o, tile, at, g)
            total = total + tile * tile
        mean = jnp.sum(total, axis=1, keepdims=True) * (1.0 / channels)
        inv_o[pl.ds(at, 16), :] = jnp.broadcast_to(lax.rsqrt(mean + 1e-06), (16, LANES))

    def spread_own(i, carry):
        start = pl.multiple_of(i * 16, 16)
        spread(own, start, start + 16)
        return carry

    load.wait()
    lax.fori_loop(0, tokens // 16, spread_own, 0)

    pl.semaphore_wait(barrier, nyc - 1 + nx - 1 + nyc + 2)

    def send(src, dst, sems, where):
        pltpu.make_async_remote_copy(
            src_ref=src, dst_ref=dst, send_sem=sems.at[0], recv_sem=sems.at[1],
            device_id=where, device_id_type=MESH,
        ).start()

    def slot_of(j):
        return pl.ds(pl.multiple_of(j * MODES, MODES), MODES)

    def few_of(j):
        return pl.ds(pl.multiple_of(j * few, few), few)

    deep = [len(quarters) * few for quarters in PARTS]

    def deep_of(h, j):
        return pl.ds(pl.multiple_of(j * deep[h], few), deep[h])

    def far_first(k, count):
        return count // 2 + (1 - 2 * lax.rem(k, 2)) * (k // 2)

    def send_row(h, src, dst, sems, up):
        def one(p, carry):
            j = lax.rem(yc + far_first(p, nyc), nyc)
            where = {"phase": above, "ctx": x * nyc + j} if up else {"ctx": x * nyc + j}
            send(src.at[deep_of(h, j)], dst.at[deep_of(h, yc)], sems, where)
            return carry
        lax.fori_loop(1, nyc + 1 if up else nyc, one, 0, unroll=True)

    def send_col(src, dst, sems):
        def one(p, carry):
            send(src, dst, sems, {"ctx": lax.rem(x + far_first(p, nx), nx) * nyc + yc})
            return carry
        lax.fori_loop(1, nx, one, 0)

    def send_line(src, dst, sems):
        def one(p, carry):
            send(src, dst, sems, {"ctx": x * nyc + lax.rem(y + far_first(p, ROWS), ROWS) * CORES + c})
            return carry
        lax.fori_loop(1, ROWS, one, 0)

    def send_act(q, start, count):
        part = pl.ds(q * wide, wide)
        rows = pl.ds(start, count)
        send(act.at[rows, part], act_z.at[rows, part], act_sem.at[q], {"phase": above})

    def send_acts(point):
        for q, start, count in PLAN[point]:
            if q >= near:
                send_act(q, start, count)

    send(blk, mate, mate_sem, {"ctx": twin})
    group = x * ROWS + y
    drain(mate, mate_sem.at[1])
    both[...] = blk[...] + mate[...]
    first_rates[c, few_of(group), :] = both[few_of(c), :]
    send_line(first_rates.at[c, few_of(group)], first_rates.at[c, few_of(group)], fy_sem)
    send(act.at[pl.ds(tokens - 16, 16)], halo, halo_sem, {"ctx": after})
    send(both.at[slot_of(c)], pair_z, pair_sem, {"phase": above})
    send(act.at[pl.ds(tokens - 16, 16), far], halo_z.at[:, far], halo_z_sem,
         {"phase": above, "ctx": after})
    send(inv_o.at[pl.ds(tokens, 16)], inv_z.at[pl.ds(0, 16)], inv_z_sem.at[1],
         {"phase": above, "ctx": after})
    send_acts(0)

    drain(halo, halo_sem.at[1])
    spread(halo, 0, 0)

    def rows_of(token, q):
        return pl.ds(pl.multiple_of(token * groups + 8 * q, 8), 8)

    def fixed(r, q):
        return slice(r * groups + 8 * q, r * groups + 8 * q + 8)

    def param(j, q):
        return slice((q * KINDS + j) * 8, (q * KINDS + j) * 8 + 8)

    far_par = pl.ds(near * KINDS * 8, (nx - near) * KINDS * 8)
    first = jnp.where(me > 0, 1.0, 0.0).astype(F32)

    def features(q, raw, scale, par, uu, qf):
        gain = par[param(0, q), :]
        taps = [par[param(1 + j, q), :] for j in range(9)]

        def normed(token):
            value = raw[rows_of(token, q), :] * scale[pl.ds(token, 1), :] * gain
            return value.astype(BF16).astype(F32)

        def one(i, carry):
            back1, back2 = carry
            for k in range(4):
                t = i * 4 + k
                now = normed(t + 16)
                feats = [
                    None if b == 0 and qf is None else
                    (taps[3 * b] * now + taps[3 * b + 1] * back1) + taps[3 * b + 2] * back2
                    for b in range(3)
                ]
                if qf is not None:
                    qf[rows_of(t, q), :] = feats[0]
                uu[rows_of(t, q), :] = (feats[1] * feats[2]).astype(BF16).astype(F32)
                back1, back2 = now, back1
            return back1, back2

        lax.fori_loop(0, tokens // 4, one, (normed(15) * first, normed(14) * first))

    def features_own(q):
        features(q, raw_o, inv_o, par_o, uu_o, qf_o if q < near else None)

    for q in PARTS[0]:
        features_own(q)

    drain(first_rates.at[0, pl.ds(0, (ROWS - 1) * few)], fy_sem.at[1])
    line = pl.ds(pl.multiple_of(x * ROWS * few, ROWS * few), ROWS * few)
    send_col(first_rates.at[c, line], first_rates.at[c, line], fx_sem)

    drain(pair_z, pair_sem.at[1])
    home = jnp.broadcast_to(jnp.where(x < near, 1.0, 0.0).astype(F32), (MODES, LANES))
    filt[c, slot_of(group), :] = jnp.where(home > 0.5, both[slot_of(c), :], pair_z[...])
    send_line(filt.at[c, slot_of(group)], filt.at[c, slot_of(group)], py_sem)
    send_acts(1)

    for q in PARTS[1]:
        features_own(q)

    drain(first_rates.at[0, pl.ds(0, (nx - 1) * ROWS * few)], fx_sem.at[1])
    send(first_rates.at[c], first_rates.at[c], fs_sem, {"ctx": twin})
    drain(first_rates.at[0], fs_sem.at[1])

    def strided(h, k, r):
        return pl.ds(r // few * deep[h] + k * few + r % few, 8, stride=CORES * deep[h])

    def end_state(h):
        for k, q in enumerate(PARTS[h]):
            decay = [
                jnp.exp(-first_rates[
                    r // few, pl.ds(q * ROWS * few + r % few, 8, stride=few), :])
                for r in range(MODES)
            ]
            for r in range(MODES):
                av[fixed(r, q), :] = decay[r]
            decay = [av[fixed(r, q), :] for r in range(MODES)]

            def one(i, state):
                for step in range(4):
                    value = uu_o[rows_of(i * 4 + step, q), :]
                    state = tuple(decay[r] * state[r] + value for r in range(MODES))
                return state

            state = lax.fori_loop(
                0, tokens // 4, one, tuple(jnp.zeros((8, LANES), F32) for _ in range(MODES))
            )
            for r in range(MODES):
                sb[h, strided(h, k, r), :] = state[r]
        send_row(h, sb.at[h], rb.at[h], row_sem.at[h], False)
        rb[h, deep_of(h, yc), :] = sb[h, deep_of(h, yc), :]

    def own_rate(h):
        return jnp.concatenate(
            [first_rates[c, few_of(q * ROWS + y), :] for q in PARTS[h]], axis=0)

    def line_sum(h):
        drain(rb.at[h, pl.ds(0, (nyc - 1) * deep[h])], row_sem.at[h, 1])
        shard_decay = jnp.exp(own_rate(h) * (-float(tokens)))
        state = jnp.zeros((deep[h], LANES), F32)
        for j in range(nyc):
            pf[h, j * deep[h]:(j + 1) * deep[h], :] = state
            state = shard_decay * state + rb[h, j * deep[h]:(j + 1) * deep[h], :]
        rt[h, 0:deep[h], :] = state
        rx[h, deep_of(h, x), :] = state
        send_col(rt.at[h, pl.ds(0, deep[h])], rx.at[h, deep_of(h, x)], tot_sem.at[h])

    def carries(h):
        drain(rx.at[h, pl.ds(0, (nx - 1) * deep[h])], tot_sem.at[h, 1])
        shard_decay = jnp.exp(own_rate(h) * (-float(tokens)))
        line_decay = jnp.exp(own_rate(h) * (-float(tokens * nyc)))
        enter = jnp.zeros((deep[h], LANES), F32)
        for k in range(nx):
            earlier = jnp.broadcast_to(jnp.where(k < x, 1.0, 0.0).astype(F32), (deep[h], LANES))
            longer = line_decay * enter + rx[h, k * deep[h]:(k + 1) * deep[h], :]
            enter = jnp.where(earlier > 0.5, longer, enter)
        for j in range(nyc):
            pb[h, j * deep[h]:(j + 1) * deep[h], :] = pf[h, j * deep[h]:(j + 1) * deep[h], :] + enter
            enter = enter * shard_decay
        send_row(h, pb.at[h], cb.at[h], car_sem.at[h], h > 0)
        if h == 0:
            cb[h, deep_of(h, yc), :] = pb[h, deep_of(h, yc), :]

    def car_slots(h):
        return cb.at[h, pl.ds(0, (nyc if h > 0 else nyc - 1) * deep[h])]

    def features_far(q):
        drain(act_z.at[:, pl.ds(q * wide, wide)], act_sem.at[q, 1])

        def spread_other(i, carry):
            start = pl.multiple_of(i * 16, 16)
            for g in range(8 * q, 8 * q + 8):
                tile = act_z[pl.ds(start, 16), g * LANES:(g + 1) * LANES].astype(F32)
                place(raw_z, tile, start + 16, g)
            return carry

        lax.fori_loop(0, tokens // 16, spread_other, 0)
        for g in range(8 * q, 8 * q + 8):
            place(raw_z, halo_z[:, g * LANES:(g + 1) * LANES].astype(F32), 0, g)
        features(q, raw_z, inv_z, par_z, uu_z, qf_z)

    def aligned(q):
        for r in range(MODES):
            at = pl.ds(q * ROWS * MODES + r, 8, stride=MODES)
            av[fixed(r, q), :] = jnp.exp(-filt[0, at, :])
            wv[fixed(r, q), :] = filt[1, at, :]

    def finish(h, k):
        q = PARTS[h][k]
        raw, uu, qf, par = (
            (raw_o, uu_o, qf_o, par_o) if q < near else (raw_z, uu_z, qf_z, par_z))
        decay = [av[fixed(r, q), :] for r in range(MODES)]
        weight = [wv[fixed(r, q), :] for r in range(MODES)]
        skip = par[param(10, q), :]

        def one(i, state):
            for step in range(4):
                t = i * 4 + step
                value = uu[rows_of(t, q), :]
                state = tuple(decay[r] * state[r] + value for r in range(MODES))
                terms = [weight[r] * state[r] for r in range(MODES)]
                while len(terms) > 1:
                    terms = [terms[2 * m] + terms[2 * m + 1] for m in range(len(terms) // 2)]
                conv = terms[0].astype(BF16).astype(F32)
                qf[rows_of(t, q), :] = (
                    raw[rows_of(t + 16, q), :]
                    + qf[rows_of(t, q), :] * (conv + skip * value))
            return state

        state = tuple(
            cb[h, strided(h, k, r), :] for r in range(MODES))

        def gather(i, carry):
            start = pl.multiple_of(i * 16, 16)
            for g in range(8 * q, 8 * q + 8):
                low = qf[pl.ds(start * groups + g, 8, stride=groups), :]
                high = qf[pl.ds((start + 8) * groups + g, 8, stride=groups), :]
                ob[pl.ds(start, 16), g * LANES:(g + 1) * LANES] = (
                    jnp.concatenate([low, high], axis=0).astype(BF16))
            return carry

        part = pl.ds(q * wide, wide)
        rows = tokens // CUTS
        for cut in range(CUTS):
            state = lax.fori_loop(cut * rows // 4, (cut + 1) * rows // 4, one, state)
            lax.fori_loop(cut * rows // 16, (cut + 1) * rows // 16, gather, 0)
            piece = pl.ds(cut * rows, rows)
            if q < near:
                send(ob.at[piece, part], out.at[piece, part], z_sem, {"phase": above})
            else:
                pltpu.make_async_copy(
                    ob.at[piece, part], out.at[piece, part], store_sem).start()

    end_state(0)
    end_state(1)
    drain(filt.at[0, pl.ds(0, (ROWS - 1) * MODES)], py_sem.at[1])
    span = pl.ds(pl.multiple_of(x * ROWS * MODES, ROWS * MODES), ROWS * MODES)
    send_col(filt.at[c, span], filt.at[c, span], px_sem)
    send(par_o.at[far_par], par_z.at[far_par], prm_sem, {"phase": above})
    send(inv_o.at[pl.ds(16, tokens)], inv_z.at[pl.ds(16, tokens)], inv_z_sem.at[0],
         {"phase": above})
    send_acts(2)
    line_sum(0)
    line_sum(1)
    send_acts(3)
    carries(0)
    drain(filt.at[0, pl.ds(0, (nx - 1) * ROWS * MODES)], px_sem.at[1])
    send(filt.at[c], filt.at[c], swap_sem, {"ctx": twin})
    carries(1)
    send_acts(4)
    drain(filt.at[0], swap_sem.at[1])
    for q in range(nx):
        aligned(q)
    drain(par_z.at[far_par], prm_sem.at[1])
    drain(halo_z.at[:, far], halo_z_sem.at[1])
    drain(inv_z.at[pl.ds(16, tokens)], inv_z_sem.at[0, 1])
    drain(inv_z.at[pl.ds(0, 16)], inv_z_sem.at[1, 1])
    for q in PARTS[1][:EARLY]:
        features_far(q)
    drain(car_slots(0), car_sem.at[0, 1])
    for k in range(len(PARTS[0])):
        finish(0, k)
    for q in PARTS[1][EARLY:]:
        features_far(q)
    drain(car_slots(1), car_sem.at[1, 1])
    for k in range(len(PARTS[1])):
        finish(1, k)

    drain(blk, mate_sem.at[0])
    drain(pair_z, pair_sem.at[0])
    drain(halo, halo_sem.at[0])
    drain(par_z.at[far_par], prm_sem.at[0])
    for q in range(near, nx):
        drain(act_z.at[:, pl.ds(q * wide, wide)], act_sem.at[q, 0])
    drain(halo_z.at[:, far], halo_z_sem.at[0])
    drain(inv_z.at[pl.ds(16, tokens)], inv_z_sem.at[0, 0])
    drain(inv_z.at[pl.ds(0, 16)], inv_z_sem.at[1, 0])
    drain(first_rates.at[0, pl.ds(0, (ROWS - 1) * few)], fy_sem.at[0])
    drain(first_rates.at[0, pl.ds(0, (nx - 1) * ROWS * few)], fx_sem.at[0])
    drain(first_rates.at[0], fs_sem.at[0])
    drain(filt.at[0, pl.ds(0, (ROWS - 1) * MODES)], py_sem.at[0])
    drain(filt.at[0, pl.ds(0, (nx - 1) * ROWS * MODES)], px_sem.at[0])
    drain(filt.at[0], swap_sem.at[0])
    for h in range(halves):
        drain(rb.at[h, pl.ds(0, (nyc - 1) * deep[h])], row_sem.at[h, 0])
        drain(rx.at[h, pl.ds(0, (nx - 1) * deep[h])], tot_sem.at[h, 0])
        drain(car_slots(h), car_sem.at[h, 0])
    drain(ob.at[:, far], store_sem)
    drain(ob.at[:, pl.ds(0, near * wide)], z_sem.at[0])
    drain(ob.at[:, pl.ds(0, near * wide)], z_sem.at[1])


def local(phases, nx, activations, norm_gain, short_taps, skip_gain, time_const, residues):
    act = activations[0]
    tokens, channels = act.shape
    groups = channels // LANES
    halves = 2
    nyc = ROWS * CORES
    most = max(len(quarters) for quarters in PARTS) * MODES // CORES
    vmem = pltpu.VMEM
    dma = pltpu.SemaphoreType.DMA
    out = pl.pallas_call(
        functools.partial(kernel, phases, nx, tokens),
        out_shape=jax.ShapeDtypeStruct((tokens, channels), BF16),
        in_specs=[
            pl.BlockSpec(memory_space=pl.ANY),
            pl.BlockSpec(memory_space=vmem),
            pl.BlockSpec(memory_space=vmem),
            pl.BlockSpec(memory_space=vmem),
            pl.BlockSpec(memory_space=vmem),
            pl.BlockSpec(memory_space=vmem),
        ],
        out_specs=pl.BlockSpec(memory_space=pl.ANY),
        scratch_shapes=[
            vmem((2 * MODES, LANES), F32),
            vmem((tokens, channels), BF16),
            vmem((tokens, channels), BF16),
            vmem((16, channels), BF16),
            vmem((16, channels), BF16),
            vmem((2 * MODES, LANES), F32),
            vmem((MODES, LANES), F32),
            vmem((2 * MODES, LANES), F32),
            vmem(((tokens + 16) * groups, LANES), F32),
            vmem(((tokens + 16) * groups, LANES), F32),
            vmem((tokens + 16, LANES), F32),
            vmem((tokens + 16, LANES), F32),
            vmem((KINDS * groups, LANES), F32),
            vmem((KINDS * groups, LANES), F32),
            vmem((tokens * groups, LANES), F32),
            vmem((tokens * groups, LANES), F32),
            vmem((tokens * groups, LANES), F32),
            vmem((tokens * groups, LANES), F32),
            vmem((CORES, groups * MODES // CORES, LANES), F32),
            vmem((2, groups * MODES, LANES), F32),
            vmem((groups * MODES, LANES), F32),
            vmem((groups * MODES, LANES), F32),
            vmem((tokens, channels), BF16),
            vmem((halves, nyc * most, LANES), F32),
            vmem((halves, nyc * most, LANES), F32),
            vmem((halves, nyc * most, LANES), F32),
            vmem((halves, nyc * most, LANES), F32),
            vmem((halves, nyc * most, LANES), F32),
            vmem((halves, most, LANES), F32),
            vmem((halves, nx * most, LANES), F32),
            dma(()),
            dma((2,)),
            dma((2,)),
            dma((2,)),
            dma((2,)),
            dma((nx, 2)),
            dma((2,)),
            dma((2, 2)),
            dma((2,)),
            dma((2,)),
            dma((2,)),
            dma((2,)),
            dma((2,)),
            dma((2,)),
            dma((halves, 2)),
            dma((halves, 2)),
            dma((halves, 2)),
            dma((2,)),
            dma(()),
        ],
        compiler_params=pltpu.CompilerParams(
            collective_id=0, has_side_effects=True, vmem_limit_bytes=56 * 1024 * 1024),
    )(act, norm_gain, short_taps[0], skip_gain, time_const[0].T, residues[0].T)
    return out[None]


def solution(mesh):
    in_specs = (
        P("phase", "ctx", None),
        P("phase", None),
        P("phase", None, None, None),
        P("phase", None),
        P("phase", "ctx", None),
        P("phase", "ctx", None),
    )
    nx = mesh.shape["ctx"] // (ROWS * CORES)
    return jax.shard_map(
        functools.partial(local, mesh.shape["phase"], nx),
        mesh=mesh, in_specs=in_specs, out_specs=P("phase", "ctx", None), check_vma=False)
```
